256 devices in a mesh: dp: 64 (over y, x_hi, z), tensor: 4 (over x_lo, core).
Axes of the slice: x: 4 (x_hi: 2, x_lo: 2; x = x_hi * 2 + x_lo), y: 4, z: 8, core: 2. Of those that a mesh axis runs over, the one named last changes fastest.
Arguments:
- tokens: bfloat16 [24576, 8192], P('dp', 'tensor'), may hold values from -6 to 6
- norm_gain: bfloat16 [8192], replicated, may hold values from 0.099609375 to 1.8984375
- q_weight: bfloat16 [8192, 2048], P('dp', 'tensor'), as said below
- key_value_weight: bfloat16 [8192, 2, 512], P('dp', None, 'tensor'), as said below
- output_weight: bfloat16 [2048, 8192], P('tensor', 'dp'), may hold values from -0.125 to 0.125
- lengths: int32 [64], P('dp'), may hold values from 1 to 384, as said below
Outputs:
- mixed: bfloat16 [24576, 8192], P('dp', 'tensor')
The draws below stay inside these ranges and needn't reach their ends.
Inputs may be any that keep to these rules, and one draw needn't show every extreme that they name: The first lengths tokens of a sequence are valid; at least one sequence has all 384 valid. `key_value_weight`: independent entries of scale 8192 ** -0.5. `q_weight`: in one draw independent entries of order 8192 ** -0.5; in the other each query head is the key projection of its group times a per-head factor of 8 to 24, plus half an independent matrix of that scale.
All inputs are finite; a program needn't handle non-finite values.
Results may differ from the reference program's by a relative error of at most 0.013.
Values may be sent and summed in bfloat16 or wider, within the bound.
A program may use at most 128 MiB of HBM per device.

```python
import jax
import jax.numpy as jnp
from jax import lax

MODEL_WIDTH = 8192
HEAD_DIM = 128
QUERY_HEADS_PART = 4
SEQUENCE_LENGTH = 384
SEQS = 64
TOKENS = 24576
KEY_VALUE_HEADS = 4
HQ = 16


def shared_keys(key):
    return jax.random.normal(jax.random.fold_in(key, 101), (MODEL_WIDTH, KEY_VALUE_HEADS * HEAD_DIM), jnp.float32) * MODEL_WIDTH ** (-0.5)


def draw_key_value_weight(key, part):
    rotary_base = shared_keys(key)
    key = jax.random.fold_in(key, 2)
    value_rows = jax.random.normal(key, (MODEL_WIDTH, KEY_VALUE_HEADS * HEAD_DIM), jnp.float32) * MODEL_WIDTH ** (-0.5)
    return jnp.stack([rotary_base, value_rows], axis=1).astype(jnp.bfloat16)


def draw_q_weight(key, part):
    key = jax.random.fold_in(key, 1)
    own = jax.random.normal(key, (MODEL_WIDTH, HQ * HEAD_DIM), jnp.float32) * MODEL_WIDTH ** (-0.5)
    weight = own
    return weight.astype(jnp.bfloat16)


def draw_lengths(key, part):
    key = jax.random.fold_in(key, 3)
    value_rows = jax.random.randint(key, (SEQS,), 1, SEQUENCE_LENGTH + 1)
    chosen = jax.random.randint(jax.random.fold_in(key, 4), (), 0, SEQS)
    return jnp.where(jnp.arange(SEQS) == chosen, SEQUENCE_LENGTH, value_rows).astype(jnp.int32)


def shard_levels(key, extent, pieces, smallest, top_value):
    def one(dim, blocks):
        draws = jax.random.uniform(jax.random.fold_in(jax.random.fold_in(key, 6), dim), (blocks,), jnp.float32, smallest / len(pieces), top_value / len(pieces))
        return jnp.repeat(jnp.exp(draws), extent[dim] // blocks).reshape((-1,) + (1,) * (len(extent) - dim - 1))

    level = one(*pieces[0])
    for cut in pieces[1:]:
        level = level * one(*cut)
    return level


def noise(own_key, extent, width, most, cuts=(), held_as=jnp.bfloat16):
    entries = width * jax.random.normal(own_key, extent, jnp.float32)
    if cuts:
        entries = entries * shard_levels(own_key, extent, cuts, -0.22, 0.18)
    return jnp.clip(entries, -most, most).astype(held_as)


def setup_inputs(seed: int = 0) -> dict:
    keys = jax.random.split(jax.random.key(seed), 7)
    return {
        "tokens": noise(keys[0], (TOKENS, MODEL_WIDTH), 1.0, 6.0, ((0, 64), (1, 4))),
        "norm_gain": jnp.clip(1.0 + 0.18 * jax.random.normal(keys[1], (MODEL_WIDTH,), jnp.float32), 0.099609375, 1.8984375).astype(jnp.bfloat16),
        "q_weight": draw_q_weight(jax.random.fold_in(keys[6], 71), 0),
        "key_value_weight": draw_key_value_weight(jax.random.fold_in(keys[6], 71), 0),
        "output_weight": noise(keys[4], (HQ * HEAD_DIM, MODEL_WIDTH), (HQ * HEAD_DIM) ** -0.5, 0.125, ((0, 4), (1, 64))),
        "lengths": draw_lengths(jax.random.fold_in(keys[6], 71), 0),
    }


def apply_rotary(value_rows, token_positions):
    half = value_rows.shape[-1] // 2
    freqs = 500000.0 ** (-(jnp.arange(half, dtype=jnp.float32) * 2.0 / value_rows.shape[-1]))
    angles = token_positions[:, None] * freqs[None, :]
    cosine = jnp.cos(angles)[:, None, :]
    sine = jnp.sin(angles)[:, None, :]
    first = value_rows[..., :half]
    second = value_rows[..., half:]
    return jnp.concatenate([first * cosine - second * sine, second * cosine + first * sine], axis=-1)

def reference(tokens, norm_gain, q_weight, key_value_weight, output_weight, lengths):
    key_value_flat = key_value_weight.reshape(MODEL_WIDTH, 2 * KEY_VALUE_HEADS * HEAD_DIM)
    output_groups = output_weight.reshape(KEY_VALUE_HEADS, QUERY_HEADS_PART * HEAD_DIM, MODEL_WIDTH)
    token_positions = jnp.arange(SEQUENCE_LENGTH, dtype=jnp.float32)
    rows = jnp.arange(SEQUENCE_LENGTH, dtype=jnp.int32)

    def one_sequence(item):
        block, length = item
        xf = block.astype(jnp.float32)
        msq = lax.optimization_barrier(jnp.mean(xf * xf, axis=-1, keepdims=True))
        normed_input = (xf * lax.rsqrt(msq + 1e-05) * norm_gain.astype(jnp.float32)).astype(jnp.bfloat16)
        query_rows = jnp.dot(normed_input, q_weight, preferred_element_type=jnp.float32).reshape(SEQUENCE_LENGTH, HQ, HEAD_DIM)
        key_value_pair = jnp.dot(normed_input, key_value_flat, preferred_element_type=jnp.float32).reshape(SEQUENCE_LENGTH, 2, KEY_VALUE_HEADS, HEAD_DIM)
        rotated_query = apply_rotary(query_rows, token_positions).astype(jnp.bfloat16).reshape(SEQUENCE_LENGTH, KEY_VALUE_HEADS, QUERY_HEADS_PART, HEAD_DIM)
        rk = apply_rotary(key_value_pair[:, 0], token_positions).astype(jnp.bfloat16)
        rv = key_value_pair[:, 1].astype(jnp.bfloat16)
        scores = jnp.einsum('ighd,jgd->ghij', rotated_query.astype(jnp.float32), rk.astype(jnp.float32)) / jnp.sqrt(jnp.float32(HEAD_DIM))
        keep = (rows[None, :] <= rows[:, None]) & (rows[None, :] < length)
        scores = jnp.where(keep[None, None], scores, jnp.float32(-1e+30))
        top = lax.optimization_barrier(jnp.max(scores, axis=-1, keepdims=True))
        expo = jnp.exp(scores - top)
        weights = (expo / lax.optimization_barrier(jnp.sum(expo, axis=-1, keepdims=True))).astype(jnp.bfloat16)
        attended_output = jnp.einsum('ghij,jgd->ighd', weights.astype(jnp.float32), rv.astype(jnp.float32)).astype(jnp.bfloat16)
        attended_output = attended_output.reshape(SEQUENCE_LENGTH, KEY_VALUE_HEADS, QUERY_HEADS_PART * HEAD_DIM)
        parts = jnp.einsum('lgc,gcd->gld', attended_output.astype(jnp.float32), output_groups.astype(jnp.float32)).astype(jnp.bfloat16)
        parts = lax.optimization_barrier(parts)
        total = xf + lax.optimization_barrier(jnp.sum(parts.astype(jnp.float32), axis=0))
        return total.astype(jnp.bfloat16)
    mixed = lax.map(one_sequence, (tokens.reshape(SEQS, SEQUENCE_LENGTH, MODEL_WIDTH), lengths))
    return mixed.reshape(TOKENS, MODEL_WIDTH)
```

```python
import functools

import jax
import jax.numpy as jnp
import numpy as np
from jax import lax
from jax.experimental import pallas as pl
from jax.experimental.pallas import tpu as pltpu
from jax.sharding import PartitionSpec as P

MESH = pl.DeviceIdType.MESH
SEQ = 384
HEAD = 128
HEADS = 4
FEATS = 2048
NY, NH, NZ = 4, 2, 8


def rotary_tables():
    half = HEAD // 2
    freqs = 500000.0 ** (-(np.arange(half, dtype=np.float64) * 2.0 / HEAD))
    angles = np.arange(SEQ, dtype=np.float64)[:, None] * freqs[None, :]
    cosine, sine = np.cos(angles), np.sin(angles)
    return (
        np.concatenate([cosine, cosine], axis=1).astype(np.float32),
        np.concatenate([-sine, sine], axis=1).astype(np.float32),
    )


def device(y, h, z, l, c):
    return (y * (NH * NZ) + h * NZ + z, l * 2 + c)


def kernel(
    tok, gain, w1_own, wo_own, len_own, cos, sin, out,
    xb, w1, wo, ab, aout, lenb, acc, ssq,
    t_ss, t_rs, t_fs, l_sem, e_ss, e_rs, n_ss, n_rs,
    z_ss, z_rs, y_ss, y_rs, c_ss, c_rs,
    ox_ss, ox_rs, oy_ss, oy_rs, oz_ss, oz_rs,
    a_ss, a_rs, b_ss, b_rs,
):
    dp = lax.axis_index("dp")
    tensor = lax.axis_index("tensor")
    y, h, z = dp // (NH * NZ), (dp // NZ) % NH, dp % NZ
    l, c = tensor // 2, tensor % 2
    x = 2 * h + l
    main = c == h
    yp, yn = (y + 1) % NY, (y + NY - 1) % NY

    def zat(k):
        return (z + k + NZ) % NZ

    def at_x(xx, cc):
        return device(y, xx // 2, z, xx % 2, cc)

    def remote(src, dst, ss, rs, dev):
        return pltpu.make_async_remote_copy(
            src_ref=src, dst_ref=dst, send_sem=ss, recv_sem=rs, device_id=dev, device_id_type=MESH
        )

    xnext, xprev = (x + 1) % 4, (x + 3) % 4
    sibling = device(y, h, z, l, 1 - c)
    z_dev = (device(y, h, zat(1), l, c), device(y, h, zat(-1), l, c))
    y_dev = (device(yp, h, z, l, c), device(yn, h, z, l, c))

    barrier = pltpu.get_barrier_semaphore()
    partners = [sibling, *z_dev, *y_dev]
    for k in (1, 2, 3):
        for cc in (0, 1):
            partners.append(at_x((x + k) % 4, cc))
    for p in partners:
        pl.semaphore_signal(barrier, inc=1, device_id=p, device_id_type=MESH)
    pl.semaphore_wait(barrier, len(partners))

    me1 = y * 16 + c * 8 + z
    partner = device(y, 1 - h, z, l, 1 - c)
    exchange = remote(w1_own, w1.at[y * 16 + (1 - c) * 8 + z], e_ss.at[0], e_rs.at[0], partner)
    exchange_in = remote(w1_own, w1.at[me1], e_ss.at[0], e_rs.at[0], partner)
    len_out = remote(len_own, lenb, n_ss.at[0], n_rs.at[0], partner)
    own1 = pltpu.make_async_copy(w1_own, w1.at[me1], l_sem.at[0])
    own_len = pltpu.make_async_copy(len_own, lenb, l_sem.at[1])

    @pl.when(main)
    def _():
        own1.start()
        own_len.start()

    @pl.when(jnp.logical_not(main))
    def _():
        exchange.start()
        len_out.start()

    own_t = 2 * l + c
    source = own_t == y
    ox_dev = [device(y, hd, z, y // 2, y % 2) for hd in (0, 1)]
    ox_self = [jnp.logical_and(source, h == hd) for hd in (0, 1)]
    ox = [remote(wo_own, wo.at[z, h, own_t], ox_ss.at[hd], ox_rs.at[h, own_t], ox_dev[hd]) for hd in (0, 1)]
    own_o = pltpu.make_async_copy(wo_own, wo.at[z, h, own_t], l_sem.at[2])
    for hd in (0, 1):
        @pl.when(jnp.logical_not(ox_self[hd]))
        def _():
            ox[hd].start()

    @pl.when(source)
    def _():
        own_o.start()

    half = SEQ // 2

    def rows(k):
        return pl.ds(k * half, half)

    r = (x + 4 - 2 * c) % 4
    up = jnp.logical_or(r == 1, r == 2)
    fwd_half = jnp.where(r >= 2, 1, 0)

    def tok_copy(dst_x, k, i):
        return remote(tok.at[rows(k)], xb.at[own_t, rows(k)], t_ss.at[i, k], t_rs.at[own_t, k], at_x(dst_x, h))

    pair_x = jnp.where(l == 0, xnext, xprev)
    outer_x = jnp.where(l == 0, xprev, xnext)
    own_tok = pltpu.make_async_copy(tok, xb.at[own_t], l_sem.at[3])
    tok_copy(pair_x, 0, 0).start()
    tok_copy(outer_x, 1, 1).start()
    tok_copy(pair_x, 1, 0).start()
    tok_copy(outer_x, 0, 1).start()

    @pl.when(main)
    def _():
        own_tok.start()

    @pl.when(jnp.logical_not(main))
    def _():
        tok_copy(x, 0, 2).start()
        tok_copy(x, 1, 2).start()

    def got_tok(f, k):
        return remote(tok.at[rows(k)], xb.at[f, rows(k)], t_ss.at[0, k], t_rs.at[f, k], sibling)

    near_pair = jnp.where(jnp.logical_or(r == 0, r == 2), 1, 0)
    fwd_x = jnp.where(up, xnext, xprev)

    def tok_forward(j):
        f = 2 * near_pair + j
        piece = xb.at[f, pl.ds(pl.multiple_of(fwd_half * half, half), half)]
        return remote(piece, piece, t_fs.at[j], t_rs.at[f, fwd_half], at_x(fwd_x, c))

    def z_piece(origin, s, d):
        b = w1.at[y * 16 + c * 8 + origin]
        if s == 4:
            b = b.at[pl.ds(64 * d, 64)]
        return b

    def w1_z(s, d):
        origin = zat(-(s - 1)) if d == 0 else zat(s - 1)
        b = z_piece(origin, s, d)
        return remote(b, b, z_ss.at[d, s - 1], z_rs.at[d, s - 1], z_dev[d])

    def w1_z_in(s, d):
        origin = zat(-s) if d == 0 else zat(s)
        b = z_piece(origin, s, d)
        return remote(b, b, z_ss.at[d, s - 1], z_rs.at[d, s - 1], z_dev[d])

    @pl.when(main)
    def _():
        own1.wait()

    @pl.when(jnp.logical_not(main))
    def _():
        exchange_in.wait_recv()

    for d in (0, 1):
        w1_z(1, d).start()

    rel = (y + NY - own_t) % NY

    def oy(d, k):
        b = wo.at[z, k]
        return remote(b, b, oy_ss.at[d, k], oy_rs.at[k], y_dev[d])

    @pl.when(rel == 0)
    def _():
        own_o.wait()
        for hs in (0, 1):
            for t in range(4):
                @pl.when(jnp.logical_not(jnp.logical_and(hs == h, t == own_t)))
                def _():
                    remote(wo_own, wo.at[z, hs, t], ox_ss.at[0], ox_rs.at[hs, t], sibling).wait_recv()
        oy(0, 0).start()
        oy(1, 1).start()
        oy(0, 1).start()
        oy(1, 0).start()

    for s in (2, 3, 4):
        for d in (0, 1):
            w1_z_in(s - 1, d).wait_recv()
            w1_z(s, d).start()

    @pl.when(rel == 1)
    def _():
        oy(0, 0).wait_recv()
        oy(0, 0).start()

    @pl.when(rel == 3)
    def _():
        oy(0, 1).wait_recv()
        oy(1, 1).start()

    for j in (0, 1):
        got_tok(2 * near_pair + j, fwd_half).wait_recv()
        tok_forward(j).start()

    for d in (0, 1):
        w1_z_in(4, d).wait_recv()

    def plane(yy, core, k=None):
        if k is None:
            return w1.at[pl.ds(yy * 16 + core * 8, 8)]
        return w1.at[pl.ds(yy * 16 + core * 8 + 4 * k, 4)]

    def share(b, i):
        return remote(b, b, c_ss.at[i], c_rs.at[i], sibling)

    def w1_y(d, k):
        b = plane(y, c, k)
        return remote(b, b, y_ss.at[d, k], y_rs.at[d, k], y_dev[d])

    def w1_y_fwd(d):
        b = plane(yn if d == 0 else yp, c, d)
        return remote(b, b, y_ss.at[d, 2], y_rs.at[d, 2], y_dev[d])

    def w1_y_in(d, k):
        yy = yn if d == 0 else yp
        b = plane(yy, c, k)
        return remote(b, b, y_ss.at[d, k], y_rs.at[d, k], y_dev[d])

    yf = (y + 2) % NY

    def w1_y_far(d):
        b = plane(yf, c, d)
        return remote(b, b, y_ss.at[d, 2], y_rs.at[d, 2], y_dev[d])

    w1_y(0, 0).start()
    w1_y(1, 1).start()
    w1_y(0, 1).start()
    w1_y(1, 0).start()
    share(plane(y, c), 0).start()

    def oz_out(s, d, k):
        origin = zat(-(s - 1)) if d == 0 else zat(s - 1)
        b = wo.at[origin, k]
        return remote(b, b, oz_ss.at[d, s - 1, k], oz_rs.at[d, s - 1, k], z_dev[d])

    def oz_in(s, d, k):
        origin = zat(-s) if d == 0 else zat(s)
        b = wo.at[origin, k]
        return remote(b, b, oz_ss.at[d, s - 1, k], oz_rs.at[d, s - 1, k], z_dev[d])

    @pl.when(rel == 1)
    def _():
        oy(0, 1).wait_recv()

    @pl.when(rel == 3)
    def _():
        oy(0, 0).wait_recv()

    @pl.when(rel == 2)
    def _():
        oy(0, 0).wait_recv()
        oy(0, 1).wait_recv()

    def oz_step(s):
        for k in (0, 1):
            for d in (0, 1):
                if s > 1:
                    oz_in(s - 1, d, k).wait_recv()
                if s < 4 or d == k:
                    oz_out(s, d, k).start()

    oz_step(1)

    acc[...] = jnp.zeros_like(acc)
    ssq[...] = jnp.zeros_like(ssq)

    def project(f):
        def body(i, _):
            cols = pl.ds(pl.multiple_of(i * 512, 512), 512)
            xf = xb[f, :, cols].astype(jnp.float32)
            sq = xf * xf
            ssq[...] += sq[:, :128] + sq[:, 128:256] + sq[:, 256:384] + sq[:, 384:]
            xg = (xf * gain[f, :, cols]).astype(jnp.bfloat16)
            w = w1[pl.ds(f * 16 + i * 4, 4)].reshape(512, 768)
            acc[...] += jnp.dot(xg, w, preferred_element_type=jnp.float32)
            return 0

        lax.fori_loop(0, 4, body, 0)

    w1_y_in(0, 0).wait_recv()
    w1_y_fwd(0).start()
    w1_y_in(1, 1).wait_recv()
    w1_y_fwd(1).start()
    share(plane(yn, c, 0), 1).start()
    share(plane(yp, c, 1), 2).start()

    oz_step(2)

    @pl.when(main)
    def _():
        own_tok.wait()

    for f in range(4):
        for k in (0, 1):
            here = jnp.logical_and(main, f == own_t)
            handed = jnp.logical_and(f // 2 == near_pair, k == fwd_half)

            @pl.when(jnp.logical_not(jnp.logical_or(here, handed)))
            def _():
                got_tok(f, k).wait_recv()

    share(plane(y, 1 - c), 0).wait_recv()
    project(y)

    w1_y_in(0, 1).wait_recv()
    share(plane(yn, c, 1), 3).start()
    w1_y_in(1, 0).wait_recv()
    share(plane(yp, c, 0), 4).start()
    share(plane(yn, 1 - c, 0), 1).wait_recv()
    share(plane(yn, 1 - c, 1), 3).wait_recv()
    project(yn)
    share(plane(yp, 1 - c, 1), 2).wait_recv()
    share(plane(yp, 1 - c, 0), 4).wait_recv()
    project(yp)

    oz_step(3)

    for d in (0, 1):
        w1_y_far(d).wait_recv()
        share(plane(yf, c, d), 5 + d).start()
    for d in (0, 1):
        share(plane(yf, 1 - c, d), 5 + d).wait_recv()
    project(yf)

    @pl.when(main)
    def _():
        own_len.wait()

    @pl.when(jnp.logical_not(main))
    def _():
        remote(len_own, lenb, n_ss.at[0], n_rs.at[0], partner).wait_recv()

    rs = lax.rsqrt(jnp.sum(ssq[...], axis=1, keepdims=True) * (1.0 / 8192.0) + 1e-05)

    def rotate(v):
        return (v * cos[...] + pltpu.roll(v, 64, 1) * sin[...]).astype(jnp.bfloat16)

    rk = rotate(acc[:, 512:640] * rs)
    rv = (acc[:, 640:768] * rs).astype(jnp.bfloat16)
    i_pos = lax.broadcasted_iota(jnp.int32, (SEQ, SEQ), 0)
    j_pos = lax.broadcasted_iota(jnp.int32, (SEQ, SEQ), 1)
    keep = jnp.logical_and(j_pos <= i_pos, j_pos < lenb[0:1, 0:1])
    scale = 1.0 / float(np.sqrt(128.0))
    t_here = 2 * l + h

    def a_self(ld):
        return jnp.logical_and(main, l == ld)

    def a_out(ld, hd):
        return remote(aout.at[hd], ab.at[t_here, hd], a_ss.at[ld, hd], a_rs.at[t_here, hd], device(y, c, z, ld, c))

    def a_in(t, hd):
        return remote(aout.at[hd], ab.at[t, hd], a_ss.at[0, hd], a_rs.at[t, hd], sibling)

    def b_copy(t, hd):
        return remote(ab.at[t, hd], ab.at[t, hd], b_ss.at[t, hd], b_rs.at[t, hd], sibling)

    for hd in range(HEADS):
        rq = rotate(acc[:, hd * HEAD : (hd + 1) * HEAD] * rs)
        s = lax.dot_general(rq, rk, (((1,), (1,)), ((), ())), preferred_element_type=jnp.float32) * scale
        s = jnp.where(keep, s, jnp.float32(-1e30))
        e = jnp.exp(s - jnp.max(s, axis=1, keepdims=True))
        total = jnp.sum(e, axis=1, keepdims=True)
        o = jnp.dot(e.astype(jnp.bfloat16), rv, preferred_element_type=jnp.float32) / total
        o = o.astype(jnp.bfloat16)
        aout[hd] = o
        for ld in (0, 1):
            @pl.when(jnp.logical_not(a_self(ld)))
            def _():
                a_out(ld, hd).start()

        @pl.when(main)
        def _():
            ab[t_here, hd] = o
            b_copy(t_here, hd).start()

    oz_step(4)

    for t in range(4):
        for hd in range(HEADS):
            @pl.when(jnp.logical_and(main, t != t_here))
            def _():
                a_in(t, hd).wait_recv()
                b_copy(t, hd).start()

            @pl.when(jnp.logical_not(main))
            def _():
                b_copy(t, hd).wait_recv()

    def project_out(zz):
        total = jnp.zeros((SEQ, 256), jnp.float32)
        for t in range(4):
            a = jnp.concatenate([ab[t, hd] for hd in range(HEADS)], axis=1)
            w = jnp.concatenate([wo[zz, 0, t], wo[zz, 1, t]], axis=1)
            total += jnp.dot(a, w, preferred_element_type=jnp.float32)
        for hh in (0, 1):
            cols = pl.ds(pl.multiple_of(hh * 1024 + zz * 128, 128), 128)
            out[:, cols] = (total[:, hh * 128 : (hh + 1) * 128] + tok[:, cols].astype(jnp.float32)).astype(jnp.bfloat16)

    def out_body(i, _):
        project_out((z + i + NZ - 3) % NZ)
        return 0

    lax.fori_loop(0, 7, out_body, 0)
    oz_in(4, 0, 0).wait_recv()
    oz_in(4, 1, 1).wait_recv()
    project_out(zat(4))

    @pl.when(jnp.logical_not(main))
    def _():
        exchange.wait_send()
        len_out.wait_send()
        tok_copy(x, 0, 2).wait_send()
        tok_copy(x, 1, 2).wait_send()

    for hd in (0, 1):
        @pl.when(jnp.logical_not(ox_self[hd]))
        def _():
            ox[hd].wait_send()
    for k in (0, 1):
        tok_copy(pair_x, k, 0).wait_send()
        tok_copy(outer_x, k, 1).wait_send()
        tok_forward(k).wait_send()
        w1_y_fwd(k).wait_send()
        for d in (0, 1):
            w1_y(d, k).wait_send()
            for s in (1, 2, 3):
                oz_out(s, d, k).wait_send()
        oz_out(4, k, k).wait_send()
    for s in (1, 2, 3, 4):
        for d in (0, 1):
            w1_z(s, d).wait_send()
    share(plane(y, c), 0).wait_send()
    for i in range(1, 7):
        share(plane(y, c, 0), i).wait_send()

    @pl.when(rel == 0)
    def _():
        for d in (0, 1):
            for k in (0, 1):
                oy(d, k).wait_send()

    @pl.when(rel == 1)
    def _():
        oy(0, 0).wait_send()

    @pl.when(rel == 3)
    def _():
        oy(1, 1).wait_send()

    for hd in range(HEADS):
        for ld in (0, 1):
            @pl.when(jnp.logical_not(a_self(ld)))
            def _():
                a_out(ld, hd).wait_send()

        @pl.when(main)
        def _():
            for t in range(4):
                b_copy(t, hd).wait_send()


def per_device(tokens, norm_gain, q_weight, key_value_weight, output_weight, lengths):
    w1_own = jnp.concatenate([q_weight, key_value_weight.reshape(128, 256)], axis=1)
    gain = norm_gain.astype(jnp.float32).reshape(4, 1, FEATS)
    len_own = jnp.broadcast_to(lengths.reshape(1, 1), (8, 128))
    cosine, sine = rotary_tables()
    dma = pltpu.SemaphoreType.DMA
    vmem = pl.BlockSpec(memory_space=pltpu.VMEM)
    bf16 = jnp.bfloat16
    return pl.pallas_call(
        kernel,
        out_shape=jax.ShapeDtypeStruct((SEQ, FEATS), bf16),
        in_specs=[vmem] * 7,
        out_specs=vmem,
        scratch_shapes=[
            pltpu.VMEM((4, SEQ, FEATS), bf16),
            pltpu.VMEM((64, 128, 768), bf16),
            pltpu.VMEM((NZ, 2, 4, 512, 128), bf16),
            pltpu.VMEM((4, HEADS, SEQ, HEAD), bf16),
            pltpu.VMEM((HEADS, SEQ, HEAD), bf16),
            pltpu.VMEM((8, 128), jnp.int32),
            pltpu.VMEM((SEQ, 768), jnp.float32),
            pltpu.VMEM((SEQ, 128), jnp.float32),
            dma((3, 2)), dma((4, 2)), dma((2,)), dma((4,)), dma((1,)), dma((1,)), dma((1,)), dma((1,)),
            dma((2, 4)), dma((2, 4)), dma((2, 3)), dma((2, 3)), dma((7,)), dma((7,)),
            dma((2,)), dma((2, 4)), dma((2, 2)), dma((2,)), dma((2, 4, 2)), dma((2, 4, 2)),
            dma((2, HEADS)), dma((4, HEADS)), dma((4, HEADS)), dma((4, HEADS)),
        ],
        compiler_params=pltpu.CompilerParams(
            collective_id=0, has_side_effects=True, vmem_limit_bytes=56 * 2**20
        ),
        cost_estimate=pl.CostEstimate(flops=8 * 10**9, bytes_accessed=4 * 2**20, transcendentals=600000),
    )(tokens, gain, w1_own, output_weight, len_own, jnp.asarray(cosine), jnp.asarray(sine))


def solution(mesh):
    return jax.shard_map(
        per_device,
        mesh=mesh,
        in_specs=(
            P("dp", "tensor"),
            P(),
            P("dp", "tensor"),
            P("dp", None, "tensor"),
            P("tensor", "dp"),
            P("dp"),
        ),
        out_specs=P("dp", "tensor"),
        check_vma=False,
    )
```

```python
import functools

import jax
import jax.numpy as jnp
import numpy as np
from jax import lax
from jax.experimental import pallas as pl
from jax.experimental.pallas import tpu as pltpu
from jax.sharding import PartitionSpec as P

MESH = pl.DeviceIdType.MESH
SEQ = 384
HEAD = 128
HEADS = 4
FEATS = 2048
NY, NH, NZ = 4, 2, 8


def rotary_tables():
    half = HEAD // 2
    freqs = 500000.0 ** (-(np.arange(half, dtype=np.float64) * 2.0 / HEAD))
    angles = np.arange(SEQ, dtype=np.float64)[:, None] * freqs[None, :]
    cosine, sine = np.cos(angles), np.sin(angles)
    return (
        np.concatenate([cosine, cosine], axis=1).astype(np.float32),
        np.concatenate([-sine, sine], axis=1).astype(np.float32),
    )


def device(y, h, z, l, c):
    return (y * (NH * NZ) + h * NZ + z, l * 2 + c)


def kernel(
    tok, gain_in, q_own, kv_own, wo_own, length, cos, sin, out,
    tok_own, gain, w1_own, len_own, xb, w1, wo, ab, aout, lenb, acc, ssq, mixed,
    t_ss, t_rs, t_fs, l_sem, e_ss, e_rs, n_ss, n_rs,
    z_ss, z_rs, y_ss, y_rs, f_ss, f_rs, c_ss, c_rs,
    ox_ss, ox_rs, oy_ss, oy_rs, oz_ss, oz_rs,
    q_ss, q_rs, gz_ss, gz_rs, gy_ss, gy_rs, x2_ss, x2_rs,
    a_ss, a_rs, b_ss, b_rs,
):
    dp = lax.axis_index("dp")
    tensor = lax.axis_index("tensor")
    y, h, z = dp // (NH * NZ), (dp // NZ) % NH, dp % NZ
    l, c = tensor // 2, tensor % 2
    x = 2 * h + l
    main = c == h
    yp, yn = (y + 1) % NY, (y + NY - 1) % NY

    def zat(k):
        return (z + k + NZ) % NZ

    def at_x(xx, cc):
        return device(y, xx // 2, z, xx % 2, cc)

    def remote(src, dst, ss, rs, dev):
        return pltpu.make_async_remote_copy(
            src_ref=src, dst_ref=dst, send_sem=ss, recv_sem=rs, device_id=dev, device_id_type=MESH
        )

    xnext, xprev = (x + 1) % 4, (x + 3) % 4
    sibling = device(y, h, z, l, 1 - c)
    z_dev = (device(y, h, zat(1), l, c), device(y, h, zat(-1), l, c))
    y_dev = (device(yp, h, z, l, c), device(yn, h, z, l, c))

    barrier = pltpu.get_barrier_semaphore()
    partners = [sibling, *z_dev, *y_dev, device((y + 2) % NY, h, z, l, c)]
    for k in (1, 2, 3):
        for cc in (0, 1):
            partners.append(at_x((x + k) % 4, cc))
    for p in partners:
        pl.semaphore_signal(barrier, inc=1, device_id=p, device_id_type=MESH)
    pl.semaphore_wait(barrier, len(partners))

    w1_own[:, :512] = q_own[...]
    w1_own[:, 512:640] = kv_own[:, 0, :]
    w1_own[:, 640:] = kv_own[:, 1, :]
    len_own[...] = jnp.full((8, 128), length[0], jnp.int32)
    me1 = y * 16 + c * 8 + z
    partner = device(y, 1 - h, z, l, 1 - c)
    exchange = remote(w1_own, w1.at[y * 16 + (1 - c) * 8 + z], e_ss.at[0], e_rs.at[0], partner)
    exchange_in = remote(w1_own, w1.at[me1], e_ss.at[0], e_rs.at[0], partner)
    len_out = remote(len_own, lenb, n_ss.at[0], n_rs.at[0], partner)
    own1 = pltpu.make_async_copy(w1_own, w1.at[me1], l_sem.at[0])
    own_len = pltpu.make_async_copy(len_own, lenb, l_sem.at[1])

    @pl.when(main)
    def _():
        own1.start()
        own_len.start()

    @pl.when(jnp.logical_not(main))
    def _():
        exchange.start()
        len_out.start()

    own_t = 2 * l + c
    rel = (y + NY - own_t) % NY
    source = rel == 0
    ox_dev = [device(y, hd, z, y // 2, y % 2) for hd in (0, 1)]
    own_u = wo.at[jnp.where(own_t == 3, NZ, z), 2 * own_t + h]
    ox = [remote(wo_own, own_u, ox_ss.at[hd], ox_rs.at[2 * own_t + h], ox_dev[hd]) for hd in (0, 1)]
    own_o = pltpu.make_async_copy(wo_own, own_u, l_sem.at[2])
    for hd in (0, 1):
        @pl.when(jnp.logical_not(jnp.logical_and(source, h == hd)))
        def _():
            ox[hd].start()

    @pl.when(source)
    def _():
        own_o.start()

    half = SEQ // 2

    def rows(k):
        return pl.ds(k * half, half)

    r = (x + 4 - 2 * c) % 4
    up = jnp.logical_or(r == 1, r == 2)
    fwd_half = jnp.where(r >= 2, 1, 0)

    def tok_copy(dst_x, k, i):
        return remote(tok.at[rows(k)], xb.at[own_t, rows(k)], t_ss.at[i, k], t_rs.at[own_t, k], at_x(dst_x, h))

    pair_x = jnp.where(l == 0, xnext, xprev)
    outer_x = jnp.where(l == 0, xprev, xnext)
    own_tok = pltpu.make_async_copy(tok, xb.at[own_t], l_sem.at[3])
    keep_tok = pltpu.make_async_copy(tok, tok_own, l_sem.at[4])
    tok_copy(pair_x, 0, 0).start()
    tok_copy(outer_x, 1, 1).start()
    tok_copy(pair_x, 1, 0).start()
    tok_copy(outer_x, 0, 1).start()

    @pl.when(main)
    def _():
        own_tok.start()

    @pl.when(jnp.logical_not(main))
    def _():
        tok_copy(x, 0, 2).start()
        tok_copy(x, 1, 2).start()

    def got_tok(f, k):
        return remote(tok.at[rows(k)], xb.at[f, rows(k)], t_ss.at[0, k], t_rs.at[f, k], sibling)

    near_pair = jnp.where(jnp.logical_or(r == 0, r == 2), 1, 0)
    fwd_x = jnp.where(up, xnext, xprev)

    def tok_forward(j):
        f = 2 * near_pair + j
        piece = xb.at[f, pl.ds(pl.multiple_of(fwd_half * half, half), half)]
        return remote(piece, piece, t_fs.at[j], t_rs.at[f, fwd_half], at_x(fwd_x, c))

    def blk(yy, origin):
        return w1.at[yy * 16 + c * 8 + origin]

    def halves(b, d):
        return b.at[pl.ds(64 * d, 64)]

    def ring(cut, piece, ss, rs):
        def at(origin, s, d):
            b = piece(origin)
            return cut(b, d) if s == 4 else b

        def send(s, d):
            b = at(zat(1 - s) if d == 0 else zat(s - 1), s, d)
            return remote(b, b, ss.at[d, s - 1], rs.at[d, s - 1], z_dev[d])

        def take(s, d):
            b = at(zat(-s) if d == 0 else zat(s), s, d)
            return remote(b, b, ss.at[d, s - 1], rs.at[d, s - 1], z_dev[d])

        return send, take

    w1_z, w1_z_in = ring(halves, lambda o: blk(y, o), z_ss, z_rs)

    def slot(i):
        return zat((0, -1, -2, -3, 1, 2, 3, 4)[i])

    def w1_y(d, i):
        b = blk(y, slot(i))
        return remote(b, b, y_ss.at[d, i], y_rs.at[d, i], y_dev[d])

    def w1_y_in(d, i):
        b = blk(yn if d == 0 else yp, slot(i))
        return remote(b, b, y_ss.at[d, i], y_rs.at[d, i], y_dev[d])

    def far_piece(yy, d, j):
        i = (0, 1 + 3 * d, 2 + 3 * d, 3 + 3 * d, 7)[j]
        b = blk(yy, slot(i))
        return halves(b, d) if j in (0, 4) else b

    def w1_f(d, j):
        b = far_piece(yn if d == 0 else yp, d, j)
        return remote(b, b, f_ss.at[d, j], f_rs.at[d, j], y_dev[d])

    yf = (y + 2) % NY

    def w1_f_in(d, j):
        b = far_piece(yf, d, j)
        return remote(b, b, f_ss.at[d, j], f_rs.at[d, j], y_dev[d])

    def share(b, i):
        return remote(b, b, c_ss.at[i], c_rs.at[i], sibling)

    def plane(yy, core):
        return w1.at[pl.ds(yy * 16 + core * 8, 8)]

    def quarter(zz, q):
        return wo.at[zz, 6 + q // 2, pl.ds((q % 2) * 256, 256)]

    def scatter(q):
        return remote(
            quarter(NZ, q), quarter(z, q), q_ss.at[q - 1], q_rs.at[0], device((y + q) % NY, h, z, l, c)
        )

    own_q = pltpu.make_async_copy(quarter(NZ, 0), quarter(z, 0), l_sem.at[5])

    def scatter_in():
        b = quarter(z, rel)
        return remote(b, b, q_ss.at[0], q_rs.at[0], sibling)

    g_z, g_z_in = ring(
        lambda b, d: b.at[pl.ds(128 * d, 128)], lambda o: quarter(o, rel), gz_ss, gz_rs
    )

    def line(yy, k):
        q = (yy + NY - own_t) % NY
        return wo.at[pl.ds(4 * k, 4), 6 + q // 2, pl.ds((q % 2) * 256, 256)]

    def g_y(d, k):
        b = line(y, k)
        return remote(b, b, gy_ss.at[d, k], gy_rs.at[d, k], y_dev[d])

    def g_y_in(d, k):
        b = line(yn if d == 0 else yp, k)
        return remote(b, b, gy_ss.at[d, k], gy_rs.at[d, k], y_dev[d])

    def g_f(d):
        b = line(yn if d == 0 else yp, d)
        return remote(b, b, gy_ss.at[d, 2], gy_rs.at[d, 2], y_dev[d])

    def g_f_in(d):
        b = line(yf, d)
        return remote(b, b, gy_ss.at[d, 2], gy_rs.at[d, 2], y_dev[d])

    def oy(d, k):
        b = wo.at[z, pl.ds(3 * h if k == 0 else 3 - 3 * h, 3)]
        return remote(b, b, oy_ss.at[d, k], oy_rs.at[k], y_dev[d])

    def oz_piece(origin, d, kind):
        if kind == 2:
            return wo.at[origin, pl.ds(3 - 3 * h, 3)]
        return wo.at[origin, pl.ds(3 * h, 3), pl.ds(256 * (d if kind == 0 else 1 - d), 256)]

    def oz(s, d, kind):
        b = oz_piece(zat(1 - s) if d == 0 else zat(s - 1), d, kind)
        return remote(b, b, oz_ss.at[d, s - 1, kind], oz_rs.at[d, s - 1, kind], z_dev[d])

    def oz_in(s, d, kind):
        b = oz_piece(zat(-s) if d == 0 else zat(s), d, kind)
        return remote(b, b, oz_ss.at[d, s - 1, kind], oz_rs.at[d, s - 1, kind], z_dev[d])

    def oz_go(s, kind):
        for d in (0, 1):
            if s > 1:
                oz_in(s - 1, d, kind).wait_recv()
            oz(s, d, kind).start()

    def g_go(s):
        for d in (0, 1):
            if s > 1:
                g_z_in(s - 1, d).wait_recv()
            g_z(s, d).start()

    half_out = wo.at[zat(4), pl.ds(3 * h, 3)]
    half_in = wo.at[zat(4), pl.ds(3 * (1 - h), 3)]
    far_out = remote(half_out, half_out, x2_ss.at[0], x2_rs.at[0], device(y, 1 - h, z, l, c))
    far_in = remote(half_in, half_in, x2_ss.at[0], x2_rs.at[0], device(y, 1 - h, z, l, c))

    @pl.when(main)
    def _():
        own1.wait()

    @pl.when(jnp.logical_not(main))
    def _():
        exchange_in.wait_recv()

    for d in (0, 1):
        w1_z(1, d).start()

    @pl.when(source)
    def _():
        own_o.wait()
        for u in range(8):
            @pl.when(u != 2 * own_t + h)
            def _():
                remote(wo_own, wo.at[z if u < 6 else NZ, u], ox_ss.at[0], ox_rs.at[u], sibling).wait_recv()
        own_q.start()
        for q in (1, 3, 2):
            scatter(q).start()
        for k in (0, 1):
            for d in (0, 1):
                oy(d, k).start()

    later = (jnp.logical_and(rel == 1, c == 1), jnp.logical_and(rel == 3, c == 0))

    def y_start(group, *ways):
        for d in (0, 1):
            @pl.when(ways[d])
            def _():
                for i in group:
                    w1_y(d, i).start()

    at_once = tuple(jnp.logical_not(v) for v in later)
    y_start((0,), *at_once)
    for s in (2, 3, 4):
        for d in (0, 1):
            w1_z_in(s - 1, d).wait_recv()
            w1_z(s, d).start()
        if s < 4:
            k = s - 2

            @pl.when(jnp.logical_or(rel == 1, rel == 3))
            def _():
                oy(0, k).wait_recv()

            for d in (0, 1):
                @pl.when(later[d])
                def _():
                    oy(d, k).start()

        if s == 2:
            y_start((1, 4), *at_once)
        if s == 3:
            y_start((0, 1, 4), *later)

            @pl.when(jnp.logical_not(source))
            def _():
                scatter_in().wait_recv()

            @pl.when(source)
            def _():
                own_q.wait()

            g_go(1)

    g_go(2)
    for i in (2, 5, 3, 6):
        for d in (0, 1):
            w1_y(d, i).start()

    for d in (0, 1):
        w1_z_in(4, d).wait_recv()
    for d in (0, 1):
        w1_y(d, 7).start()
    share(plane(y, c), 0).start()
    g_go(3)

    @pl.when(rel == 2)
    def _():
        oy(0, 0).wait_recv()

    oz_go(1, 0)
    oz_go(1, 1)

    @pl.when(rel == 2)
    def _():
        oy(0, 1).wait_recv()

    oz_go(1, 2)

    def y_group(group, j):
        for d in (0, 1):
            for i in group:
                w1_y_in(d, i).wait_recv()
            w1_f(d, j).start()

    for j in (0, 1):
        got_tok(2 * near_pair + j, fwd_half).wait_recv()
        tok_forward(j).start()
    g_go(4)
    oz_go(2, 0)
    y_group((0,), 0)
    y_group((1, 4), 1)
    oz_go(3, 0)
    oz_go(2, 2)
    y_group((2, 5), 2)
    oz_go(4, 0)
    oz_go(2, 1)
    y_group((3, 6), 3)
    y_group((7,), 4)
    share(plane(yn, c), 1).start()
    share(plane(yp, c), 2).start()
    for d in (0, 1):
        g_z_in(4, d).wait_recv()
    for d in (0, 1):
        for k in (0, 1):
            g_y(d, k if d == 0 else 1 - k).start()
    gain[...] = gain_in[...].astype(jnp.float32).reshape(1, 4 * FEATS)
    acc[...] = jnp.zeros_like(acc)
    ssq[...] = jnp.zeros_like(ssq)

    def project(f):
        def body(i, _):
            cols = pl.ds(pl.multiple_of(i * 512, 512), 512)
            xf = xb[f, :, cols].astype(jnp.float32)
            sq = xf * xf
            ssq[...] += sq[:, :128] + sq[:, 128:256] + sq[:, 256:384] + sq[:, 384:]
            g = gain[:, pl.ds(pl.multiple_of(f * FEATS + i * 512, 512), 512)]
            xg = (xf * g).astype(jnp.bfloat16)
            w = w1[pl.ds(f * 16 + i * 4, 4)].reshape(512, 768)
            acc[...] += jnp.dot(xg, w, preferred_element_type=jnp.float32)
            return 0

        lax.fori_loop(0, 4, body, 0)

    keep_tok.start()

    def tokens_here(f):
        own = jnp.logical_and(main, f == own_t)

        @pl.when(own)
        def _():
            own_tok.wait()

        for k in (0, 1):
            handed = jnp.logical_and(f // 2 == near_pair, k == fwd_half)

            @pl.when(jnp.logical_not(jnp.logical_or(own, handed)))
            def _():
                got_tok(f, k).wait_recv()

    share(plane(y, 1 - c), 0).wait_recv()
    tokens_here(y)
    project(y)
    oz_go(3, 2)
    share(plane(yn, 1 - c), 1).wait_recv()
    tokens_here(yn)
    project(yn)
    oz_go(3, 1)
    share(plane(yp, 1 - c), 2).wait_recv()
    tokens_here(yp)
    project(yp)
    for d in (0, 1):
        oz_in(4, d, 0).wait_recv()
    far_out.start()

    def far_share(yy, core, d, j):
        i = (0, 1 + 3 * d, 2 + 3 * d, 3 + 3 * d, 7)[j]
        b = w1.at[yy * 16 + core * 8 + slot(i)]
        return share(halves(b, d) if j in (0, 4) else b, 3 + 5 * d + j)

    for j in range(5):
        for d in (0, 1):
            w1_f_in(d, j).wait_recv()
            far_share(yf, c, d, j).start()
    for j in range(5):
        for d in (0, 1):
            far_share(yf, 1 - c, d, j).wait_recv()
    tokens_here(yf)
    project(yf)

    @pl.when(main)
    def _():
        own_len.wait()

    @pl.when(jnp.logical_not(main))
    def _():
        remote(len_own, lenb, n_ss.at[0], n_rs.at[0], partner).wait_recv()

    rs = lax.rsqrt(jnp.sum(ssq[...], axis=1, keepdims=True) * (1.0 / 8192.0) + 1e-05)

    def rotate(v):
        return (v * cos[...] + pltpu.roll(v, 64, 1) * sin[...]).astype(jnp.bfloat16)

    rk = rotate(acc[:, 512:640] * rs)
    rv = (acc[:, 640:768] * rs).astype(jnp.bfloat16)
    i_pos = lax.broadcasted_iota(jnp.int32, (SEQ, SEQ), 0)
    j_pos = lax.broadcasted_iota(jnp.int32, (SEQ, SEQ), 1)
    keep = jnp.logical_and(j_pos <= i_pos, j_pos < lenb[0:1, 0:1])
    scale = 1.0 / float(np.sqrt(128.0))
    t_here = 2 * l + h

    def a_self(ld):
        return jnp.logical_and(main, l == ld)

    def a_out(ld, hd):
        return remote(aout.at[hd], ab.at[t_here, hd], a_ss.at[ld, hd], a_rs.at[t_here, hd], device(y, c, z, ld, c))

    def a_in(t, hd):
        return remote(aout.at[hd], ab.at[t, hd], a_ss.at[0, hd], a_rs.at[t, hd], sibling)

    def b_copy(t, hd):
        return remote(ab.at[t, hd], ab.at[t, hd], b_ss.at[t, hd], b_rs.at[t, hd], sibling)

    for hd in range(HEADS):
        rq = rotate(acc[:, hd * HEAD : (hd + 1) * HEAD] * rs)
        s = lax.dot_general(rq, rk, (((1,), (1,)), ((), ())), preferred_element_type=jnp.float32) * scale
        s = jnp.where(keep, s, jnp.float32(-1e30))
        e = jnp.exp(s - jnp.max(s, axis=1, keepdims=True))
        total = jnp.sum(e, axis=1, keepdims=True)
        o = jnp.dot(e.astype(jnp.bfloat16), rv, preferred_element_type=jnp.float32) / total
        o = o.astype(jnp.bfloat16)
        aout[hd] = o
        for ld in (0, 1):
            @pl.when(jnp.logical_not(a_self(ld)))
            def _():
                a_out(ld, hd).start()

        @pl.when(main)
        def _():
            ab[t_here, hd] = o
            b_copy(t_here, hd).start()

        if hd == 1:
            for d in (0, 1):
                g_y_in(d, d).wait_recv()
                g_f(d).start()

    def attended_here(t):
        for hd in range(HEADS):
            @pl.when(jnp.logical_and(main, t != t_here))
            def _():
                a_in(t, hd).wait_recv()
                b_copy(t, hd).start()

            @pl.when(jnp.logical_not(main))
            def _():
                b_copy(t, hd).wait_recv()

    def product(zz, t):
        a = jnp.concatenate([ab[t, hd] for hd in range(HEADS)], axis=1)
        w = jnp.concatenate([wo[zz, 2 * t], wo[zz, 2 * t + 1]], axis=1)
        return jnp.dot(a, w, preferred_element_type=jnp.float32)

    def start_out(zz, _):
        for hh in (0, 1):
            cols = pl.ds(pl.multiple_of(hh * 1024 + zz * 128, 128), 128)
            mixed[zz, :, hh * 128 : (hh + 1) * 128] = tok_own[:, cols].astype(jnp.float32)
        return 0

    keep_tok.wait()
    lax.fori_loop(0, NZ, start_out, 0)
    for i in range(3):
        t = (t_here + i) % 3
        attended_here(t)

        def near_body(j, _, t=t):
            zz = (z + j + NZ - 2) % NZ
            mixed[zz] += product(zz, t)
            return 0

        lax.fori_loop(0, 5, near_body, 0)
    attended_here(3)
    for d in (0, 1):
        for kind in (1, 2):
            oz_in(3, d, kind).wait_recv()
    far_in.wait_recv()

    def rest_body(j, _):
        zz = (z + j + 3) % NZ
        mixed[zz] += product(zz, 0) + product(zz, 1) + product(zz, 2)
        return 0

    lax.fori_loop(0, 3, rest_body, 0)
    for d in (0, 1):
        g_y_in(d, 1 - d).wait_recv()
        g_f_in(d).wait_recv()

    def last_body(zz, _):
        total = mixed[zz] + product(zz, 3)
        for hh in (0, 1):
            cols = pl.ds(pl.multiple_of(hh * 1024 + zz * 128, 128), 128)
            out[:, cols] = total[:, hh * 128 : (hh + 1) * 128].astype(jnp.bfloat16)
        return 0

    lax.fori_loop(0, NZ, last_body, 0)

    @pl.when(jnp.logical_not(main))
    def _():
        exchange.wait_send()
        len_out.wait_send()
        tok_copy(x, 0, 2).wait_send()
        tok_copy(x, 1, 2).wait_send()

    for hd in (0, 1):
        @pl.when(jnp.logical_not(jnp.logical_and(source, h == hd)))
        def _():
            ox[hd].wait_send()
    for k in (0, 1):
        tok_copy(pair_x, k, 0).wait_send()
        tok_copy(outer_x, k, 1).wait_send()
        tok_forward(k).wait_send()
    for d in (0, 1):
        for i in range(8):
            w1_y(d, i).wait_send()
        for j in range(5):
            w1_f(d, j).wait_send()
            far_share(yf, c, d, j).wait_send()
        for s in (1, 2, 3, 4):
            w1_z(s, d).wait_send()
            g_z(s, d).wait_send()
        for k in (0, 1):
            g_y(d, k).wait_send()
        for s in (1, 2, 3):
            for kind in (0, 1, 2):
                oz(s, d, kind).wait_send()
        oz(4, d, 0).wait_send()
        g_f(d).wait_send()
    far_out.wait_send()
    share(plane(y, c), 0).wait_send()
    share(plane(yn, c), 1).wait_send()
    share(plane(yp, c), 2).wait_send()

    @pl.when(source)
    def _():
        for q in (1, 2, 3):
            scatter(q).wait_send()
        for d in (0, 1):
            for k in (0, 1):
                oy(d, k).wait_send()

    for k in (0, 1):
        @pl.when(jnp.logical_and(rel == 1, c == 1))
        def _():
            oy(0, k).wait_send()

        @pl.when(jnp.logical_and(rel == 3, c == 0))
        def _():
            oy(1, k).wait_send()

    for hd in range(HEADS):
        for ld in (0, 1):
            @pl.when(jnp.logical_not(a_self(ld)))
            def _():
                a_out(ld, hd).wait_send()

        @pl.when(main)
        def _():
            for t in range(4):
                b_copy(t, hd).wait_send()


def per_device(tokens, norm_gain, q_weight, key_value_weight, output_weight, lengths):
    cosine, sine = rotary_tables()
    dma = pltpu.SemaphoreType.DMA
    vmem = pl.BlockSpec(memory_space=pltpu.VMEM)
    bf16 = jnp.bfloat16
    return pl.pallas_call(
        kernel,
        out_shape=jax.ShapeDtypeStruct((SEQ, FEATS), bf16),
        in_specs=[pl.BlockSpec(memory_space=pl.ANY)] + [vmem] * 4 + [pl.BlockSpec(memory_space=pltpu.SMEM)] + [vmem] * 2,
        out_specs=vmem,
        scratch_shapes=[
            pltpu.VMEM((SEQ, FEATS), bf16),
            pltpu.VMEM((1, 4 * FEATS), jnp.float32),
            pltpu.VMEM((128, 768), bf16),
            pltpu.VMEM((8, 128), jnp.int32),
            pltpu.VMEM((4, SEQ, FEATS), bf16),
            pltpu.VMEM((64, 128, 768), bf16),
            pltpu.VMEM((NZ + 1, 8, 512, 128), bf16),
            pltpu.VMEM((4, HEADS, SEQ, HEAD), bf16),
            pltpu.VMEM((HEADS, SEQ, HEAD), bf16),
            pltpu.VMEM((8, 128), jnp.int32),
            pltpu.VMEM((SEQ, 768), jnp.float32),
            pltpu.VMEM((SEQ, 128), jnp.float32),
            pltpu.VMEM((NZ, SEQ, 256), jnp.float32),
            dma((3, 2)), dma((4, 2)), dma((2,)), dma((6,)), dma((1,)), dma((1,)), dma((1,)), dma((1,)),
            dma((2, 4)), dma((2, 4)), dma((2, 8)), dma((2, 8)), dma((2, 5)), dma((2, 5)), dma((13,)), dma((13,)),
            dma((2,)), dma((8,)), dma((2, 2)), dma((2,)), dma((2, 4, 3)), dma((2, 4, 3)),
            dma((3,)), dma((1,)), dma((2, 4)), dma((2, 4)), dma((2, 3)), dma((2, 3)), dma((1,)), dma((1,)),
            dma((2, HEADS)), dma((4, HEADS)), dma((4, HEADS)), dma((4, HEADS)),
        ],
        compiler_params=pltpu.CompilerParams(
            collective_id=0, has_side_effects=True, vmem_limit_bytes=56 * 2**20
        ),
        cost_estimate=pl.CostEstimate(flops=8 * 10**9, bytes_accessed=4 * 2**20, transcendentals=600000),
    )(tokens, norm_gain, q_weight, key_value_weight, output_weight, lengths, jnp.asarray(cosine), jnp.asarray(sine))


def solution(mesh):
    return jax.shard_map(
        per_device,
        mesh=mesh,
        in_specs=(
            P("dp", "tensor"),
            P(),
            P("dp", "tensor"),
            P("dp", None, "tensor"),
            P("tensor", "dp"),
            P("dp"),
        ),
        out_specs=P("dp", "tensor"),
        check_vma=False,
    )
```

```python
import functools

import jax
import jax.numpy as jnp
import numpy as np
from jax import lax
from jax.experimental import pallas as pl
from jax.experimental.pallas import tpu as pltpu
from jax.sharding import PartitionSpec as P

MESH = pl.DeviceIdType.MESH
SEQ = 384
HEAD = 128
HEADS = 4
FEATS = 2048
NY, NH, NZ = 4, 2, 8


def rotary_tables():
    half = HEAD // 2
    freqs = 500000.0 ** (-(np.arange(half, dtype=np.float64) * 2.0 / HEAD))
    angles = np.arange(SEQ, dtype=np.float64)[:, None] * freqs[None, :]
    cosine, sine = np.cos(angles), np.sin(angles)
    return (
        np.concatenate([cosine, cosine], axis=1).astype(np.float32),
        np.concatenate([-sine, sine], axis=1).astype(np.float32),
    )


def device(y, h, z, l, c):
    return (y * (NH * NZ) + h * NZ + z, l * 2 + c)


def kernel(
    tok, gain_in, q_own, kv_own, wo_own, length, cos, sin, out,
    tok_own, gain, w1_own, len_own, xb, w1, wo, ab, aout, lenb, acc, ssq, scaled, mixed,
    t_ss, t_rs, t_fs, l_sem, e_ss, e_rs, n_ss, n_rs,
    z_ss, z_rs, y_ss, y_rs, f_ss, f_rs, c_ss, c_rs,
    ox_ss, ox_rs, oy_ss, oy_rs, oz_ss, oz_rs,
    q_ss, q_rs, gz_ss, gz_rs, gy_ss, gy_rs, x2_ss, x2_rs,
    a_ss, a_rs, b_ss, b_rs,
):
    dp = lax.axis_index("dp")
    tensor = lax.axis_index("tensor")
    y, h, z = dp // (NH * NZ), (dp // NZ) % NH, dp % NZ
    l, c = tensor // 2, tensor % 2
    x = 2 * h + l
    main = c == h
    yp, yn = (y + 1) % NY, (y + NY - 1) % NY

    def zat(k):
        return (z + k + NZ) % NZ

    def at_x(xx, cc):
        return device(y, xx // 2, z, xx % 2, cc)

    def remote(src, dst, ss, rs, dev):
        return pltpu.make_async_remote_copy(
            src_ref=src, dst_ref=dst, send_sem=ss, recv_sem=rs, device_id=dev, device_id_type=MESH
        )

    xnext, xprev = (x + 1) % 4, (x + 3) % 4
    sibling = device(y, h, z, l, 1 - c)
    z_dev = (device(y, h, zat(1), l, c), device(y, h, zat(-1), l, c))
    y_dev = (device(yp, h, z, l, c), device(yn, h, z, l, c))

    barrier = pltpu.get_barrier_semaphore()
    partners = [sibling, *z_dev, *y_dev, device((y + 2) % NY, h, z, l, c)]
    for k in (1, 2, 3):
        for cc in (0, 1):
            partners.append(at_x((x + k) % 4, cc))
    for p in partners:
        pl.semaphore_signal(barrier, inc=1, device_id=p, device_id_type=MESH)
    w1_own[:, :512] = q_own[...]
    w1_own[:, 512:640] = kv_own[:, 0, :]
    w1_own[:, 640:] = kv_own[:, 1, :]
    len_own[...] = jnp.full((8, 128), length[0], jnp.int32)
    pl.semaphore_wait(barrier, len(partners))

    me1 = y * 16 + c * 8 + z
    partner = device(y, 1 - h, z, l, 1 - c)
    exchange = remote(w1_own, w1.at[y * 16 + (1 - c) * 8 + z], e_ss.at[0], e_rs.at[0], partner)
    exchange_in = remote(w1_own, w1.at[me1], e_ss.at[0], e_rs.at[0], partner)
    len_out = remote(len_own, lenb, n_ss.at[0], n_rs.at[0], partner)
    own1 = pltpu.make_async_copy(w1_own, w1.at[me1], l_sem.at[0])
    own_len = pltpu.make_async_copy(len_own, lenb, l_sem.at[1])

    @pl.when(main)
    def _():
        own1.start()
        own_len.start()

    @pl.when(jnp.logical_not(main))
    def _():
        exchange.start()
        len_out.start()

    own_t = 2 * l + c
    rel = (y + NY - own_t) % NY
    source = rel == 0
    ox_dev = [device(y, hd, z, y // 2, y % 2) for hd in (0, 1)]
    own_u = wo.at[jnp.where(own_t == 3, NZ, z), 2 * own_t + h]
    ox = [remote(wo_own, own_u, ox_ss.at[hd], ox_rs.at[2 * own_t + h], ox_dev[hd]) for hd in (0, 1)]
    own_o = pltpu.make_async_copy(wo_own, own_u, l_sem.at[2])
    for hd in (0, 1):
        @pl.when(jnp.logical_not(jnp.logical_and(source, h == hd)))
        def _():
            ox[hd].start()

    @pl.when(source)
    def _():
        own_o.start()

    half = SEQ // 2

    def rows(k):
        return pl.ds(k * half, half)

    r = (x + 4 - 2 * c) % 4
    up = jnp.logical_or(r == 1, r == 2)
    fwd_half = jnp.where(r >= 2, 1, 0)

    def tok_copy(dst_x, k, i):
        return remote(tok.at[rows(k)], xb.at[own_t, rows(k)], t_ss.at[i, k], t_rs.at[own_t, k], at_x(dst_x, h))

    pair_x = jnp.where(l == 0, xnext, xprev)
    outer_x = jnp.where(l == 0, xprev, xnext)
    own_tok = pltpu.make_async_copy(tok, xb.at[own_t], l_sem.at[3])
    keep_tok = pltpu.make_async_copy(tok, tok_own, l_sem.at[4])
    tok_copy(pair_x, 0, 0).start()
    tok_copy(outer_x, 1, 1).start()
    tok_copy(pair_x, 1, 0).start()
    tok_copy(outer_x, 0, 1).start()

    @pl.when(main)
    def _():
        own_tok.start()

    @pl.when(jnp.logical_not(main))
    def _():
        tok_copy(x, 0, 2).start()
        tok_copy(x, 1, 2).start()

    def got_tok(f, k):
        return remote(tok.at[rows(k)], xb.at[f, rows(k)], t_ss.at[0, k], t_rs.at[f, k], sibling)

    near_pair = jnp.where(jnp.logical_or(r == 0, r == 2), 1, 0)
    fwd_x = jnp.where(up, xnext, xprev)

    def tok_forward(j):
        f = 2 * near_pair + j
        piece = xb.at[f, pl.ds(pl.multiple_of(fwd_half * half, half), half)]
        return remote(piece, piece, t_fs.at[j], t_rs.at[f, fwd_half], at_x(fwd_x, c))

    def blk(yy, origin):
        return w1.at[yy * 16 + c * 8 + origin]

    def halves(b, d):
        return b.at[pl.ds(64 * d, 64)]

    def ring(cut, piece, ss, rs):
        def at(origin, s, d):
            b = piece(origin)
            return cut(b, d) if s == 4 else b

        def send(s, d):
            b = at(zat(1 - s) if d == 0 else zat(s - 1), s, d)
            return remote(b, b, ss.at[d, s - 1], rs.at[d, s - 1], z_dev[d])

        def take(s, d):
            b = at(zat(-s) if d == 0 else zat(s), s, d)
            return remote(b, b, ss.at[d, s - 1], rs.at[d, s - 1], z_dev[d])

        return send, take

    w1_z, w1_z_in = ring(halves, lambda o: blk(y, o), z_ss, z_rs)

    def slot(i):
        return zat((0, -1, -2, -3, 1, 2, 3, 4)[i])

    def w1_y(d, i):
        b = blk(y, slot(i))
        return remote(b, b, y_ss.at[d, i], y_rs.at[d, i], y_dev[d])

    def w1_y_in(d, i):
        b = blk(yn if d == 0 else yp, slot(i))
        return remote(b, b, y_ss.at[d, i], y_rs.at[d, i], y_dev[d])

    def far_piece(yy, d, j):
        i = (0, 1 + 3 * d, 2 + 3 * d, 3 + 3 * d, 7)[j]
        b = blk(yy, slot(i))
        return halves(b, d) if j in (0, 4) else b

    def w1_f(d, j):
        b = far_piece(yn if d == 0 else yp, d, j)
        return remote(b, b, f_ss.at[d, j], f_rs.at[d, j], y_dev[d])

    yf = (y + 2) % NY

    def w1_f_in(d, j):
        b = far_piece(yf, d, j)
        return remote(b, b, f_ss.at[d, j], f_rs.at[d, j], y_dev[d])

    def share(b, i):
        return remote(b, b, c_ss.at[i], c_rs.at[i], sibling)

    def plane(yy, core):
        return w1.at[pl.ds(yy * 16 + core * 8, 8)]

    def quarter(zz, q):
        return wo.at[zz, 6 + q // 2, pl.ds((q % 2) * 256, 256)]

    def scatter(q):
        return remote(
            quarter(NZ, q), quarter(z, q), q_ss.at[q - 1], q_rs.at[0], device((y + q) % NY, h, z, l, c)
        )

    own_q = pltpu.make_async_copy(quarter(NZ, 0), quarter(z, 0), l_sem.at[5])

    def scatter_in():
        b = quarter(z, rel)
        return remote(b, b, q_ss.at[0], q_rs.at[0], sibling)

    g_z, g_z_in = ring(
        lambda b, d: b.at[pl.ds(128 * d, 128)], lambda o: quarter(o, rel), gz_ss, gz_rs
    )

    def line(yy, k):
        q = (yy + NY - own_t) % NY
        return wo.at[pl.ds(4 * k, 4), 6 + q // 2, pl.ds((q % 2) * 256, 256)]

    def g_y(d, k):
        b = line(y, k)
        return remote(b, b, gy_ss.at[d, k], gy_rs.at[d, k], y_dev[d])

    def g_y_in(d, k):
        b = line(yn if d == 0 else yp, k)
        return remote(b, b, gy_ss.at[d, k], gy_rs.at[d, k], y_dev[d])

    def g_f(d):
        b = line(yn if d == 0 else yp, d)
        return remote(b, b, gy_ss.at[d, 2], gy_rs.at[d, 2], y_dev[d])

    def g_f_in(d):
        b = line(yf, d)
        return remote(b, b, gy_ss.at[d, 2], gy_rs.at[d, 2], y_dev[d])

    def oy(d, k):
        b = wo.at[z, pl.ds(3 * h if k == 0 else 3 - 3 * h, 3)]
        return remote(b, b, oy_ss.at[d, k], oy_rs.at[k], y_dev[d])

    def oz_piece(origin, d, kind):
        if kind == 2:
            return wo.at[origin, pl.ds(3 - 3 * h, 3)]
        return wo.at[origin, pl.ds(3 * h, 3), pl.ds(256 * (d if kind == 0 else 1 - d), 256)]

    def oz(s, d, kind):
        b = oz_piece(zat(1 - s) if d == 0 else zat(s - 1), d, kind)
        return remote(b, b, oz_ss.at[d, s - 1, kind], oz_rs.at[d, s - 1, kind], z_dev[d])

    def oz_in(s, d, kind):
        b = oz_piece(zat(-s) if d == 0 else zat(s), d, kind)
        return remote(b, b, oz_ss.at[d, s - 1, kind], oz_rs.at[d, s - 1, kind], z_dev[d])

    def oz_go(s, kind):
        for d in (0, 1):
            if s > 1:
                oz_in(s - 1, d, kind).wait_recv()
            oz(s, d, kind).start()

    def g_go(s):
        for d in (0, 1):
            if s > 1:
                g_z_in(s - 1, d).wait_recv()
            g_z(s, d).start()

    half_out = wo.at[zat(4), pl.ds(3 * h, 3)]
    half_in = wo.at[zat(4), pl.ds(3 * (1 - h), 3)]
    far_out = remote(half_out, half_out, x2_ss.at[0], x2_rs.at[0], device(y, 1 - h, z, l, c))
    far_in = remote(half_in, half_in, x2_ss.at[0], x2_rs.at[0], device(y, 1 - h, z, l, c))

    @pl.when(main)
    def _():
        own1.wait()

    @pl.when(jnp.logical_not(main))
    def _():
        exchange_in.wait_recv()

    for d in (0, 1):
        w1_z(1, d).start()

    @pl.when(source)
    def _():
        own_o.wait()
        for u in range(8):
            @pl.when(u != 2 * own_t + h)
            def _():
                remote(wo_own, wo.at[z if u < 6 else NZ, u], ox_ss.at[0], ox_rs.at[u], sibling).wait_recv()
        own_q.start()
        for q in (1, 3, 2):
            scatter(q).start()
        for k in (0, 1):
            for d in (0, 1):
                oy(d, k).start()

    later = (jnp.logical_and(rel == 1, c == 1), jnp.logical_and(rel == 3, c == 0))

    def y_start(group, *ways):
        for d in (0, 1):
            @pl.when(ways[d])
            def _():
                for i in group:
                    w1_y(d, i).start()

    at_once = tuple(jnp.logical_not(v) for v in later)
    y_start((0,), *at_once)
    for s in (2, 3, 4):
        for d in (0, 1):
            w1_z_in(s - 1, d).wait_recv()
            w1_z(s, d).start()
        if s < 4:
            k = s - 2

            @pl.when(jnp.logical_or(rel == 1, rel == 3))
            def _():
                oy(0, k).wait_recv()

            for d in (0, 1):
                @pl.when(later[d])
                def _():
                    oy(d, k).start()

        if s == 2:
            y_start((1, 4), *at_once)
        if s == 3:
            y_start((0, 1, 4), *later)

            @pl.when(jnp.logical_not(source))
            def _():
                scatter_in().wait_recv()

            @pl.when(source)
            def _():
                own_q.wait()

            g_go(1)

    g_go(2)
    for i in (2, 5, 3, 6):
        for d in (0, 1):
            w1_y(d, i).start()

    for d in (0, 1):
        w1_z_in(4, d).wait_recv()
    for d in (0, 1):
        w1_y(d, 7).start()
    share(plane(y, c), 0).start()
    g_go(3)

    @pl.when(rel == 2)
    def _():
        oy(0, 0).wait_recv()

    oz_go(1, 0)
    oz_go(1, 1)


    def y_group(group, j):
        for d in (0, 1):
            for i in group:
                w1_y_in(d, i).wait_recv()
            w1_f(d, j).start()

    for j in (0, 1):
        got_tok(2 * near_pair + j, fwd_half).wait_recv()
        tok_forward(j).start()
    g_go(4)
    y_group((0,), 0)
    oz_go(2, 0)

    @pl.when(rel == 2)
    def _():
        oy(0, 1).wait_recv()

    oz_go(1, 2)
    y_group((1, 4), 1)
    oz_go(3, 0)
    oz_go(2, 1)
    y_group((2, 5), 2)
    y_group((3, 6), 3)
    oz_go(4, 0)
    oz_go(2, 2)
    y_group((7,), 4)
    share(plane(yn, c), 1).start()
    share(plane(yp, c), 2).start()
    for d in (0, 1):
        g_z_in(4, d).wait_recv()
    for d in (0, 1):
        for k in (0, 1):
            g_y(d, k if d == 0 else 1 - k).start()
    gain[...] = gain_in[...].astype(jnp.float32).reshape(1, 4 * FEATS)
    acc[...] = jnp.zeros_like(acc)
    ssq[...] = jnp.zeros_like(ssq)

    def project(f):
        def body(i, _):
            cols = pl.ds(pl.multiple_of(i * 512, 512), 512)
            xf = xb[f, :, cols].astype(jnp.float32)
            sq = xf * xf
            ssq[...] += sq[:, :128] + sq[:, 128:256] + sq[:, 256:384] + sq[:, 384:]
            g = gain[:, pl.ds(pl.multiple_of(f * FEATS + i * 512, 512), 512)]
            xg = (xf * g).astype(jnp.bfloat16)
            w = w1[pl.ds(f * 16 + i * 4, 4)].reshape(512, 768)
            acc[...] += jnp.dot(xg, w, preferred_element_type=jnp.float32)
            return 0

        lax.fori_loop(0, 4, body, 0)

    def prepare(f):
        def body(i, _):
            cols = pl.ds(pl.multiple_of(i * 512, 512), 512)
            xf = xb[f, :, cols].astype(jnp.float32)
            sq = xf * xf
            ssq[...] += sq[:, :128] + sq[:, 128:256] + sq[:, 256:384] + sq[:, 384:]
            g = gain[:, pl.ds(pl.multiple_of(f * FEATS + i * 512, 512), 512)]
            scaled[:, cols] = (xf * g).astype(jnp.bfloat16)
            return 0

        lax.fori_loop(0, 4, body, 0)

    def project_prepared(f):
        def body(i, _):
            cols = pl.ds(pl.multiple_of(i * 512, 512), 512)
            w = w1[pl.ds(f * 16 + i * 4, 4)].reshape(512, 768)
            acc[...] += jnp.dot(scaled[:, cols], w, preferred_element_type=jnp.float32)
            return 0

        lax.fori_loop(0, 4, body, 0)

    keep_tok.start()

    def tokens_here(f):
        own = jnp.logical_and(main, f == own_t)

        @pl.when(own)
        def _():
            own_tok.wait()

        for k in (0, 1):
            handed = jnp.logical_and(f // 2 == near_pair, k == fwd_half)

            @pl.when(jnp.logical_not(jnp.logical_or(own, handed)))
            def _():
                got_tok(f, k).wait_recv()

    share(plane(y, 1 - c), 0).wait_recv()
    tokens_here(y)
    project(y)
    oz_go(3, 1)
    share(plane(yn, 1 - c), 1).wait_recv()
    tokens_here(yn)
    project(yn)
    for d in (0, 1):
        oz_in(4, d, 0).wait_recv()
    far_out.start()
    share(plane(yp, 1 - c), 2).wait_recv()
    tokens_here(yp)
    project(yp)
    tokens_here(yf)
    prepare(yf)

    def start_out(zz, _):
        for hh in (0, 1):
            cols = pl.ds(pl.multiple_of(hh * 1024 + zz * 128, 128), 128)
            mixed[zz, :, hh * 128 : (hh + 1) * 128] = tok_own[:, cols].astype(jnp.float32)
        return 0

    keep_tok.wait()
    lax.fori_loop(0, NZ, start_out, 0)

    def far_share(yy, core, d, j):
        i = (0, 1 + 3 * d, 2 + 3 * d, 3 + 3 * d, 7)[j]
        b = w1.at[yy * 16 + core * 8 + slot(i)]
        return share(halves(b, d) if j in (0, 4) else b, 3 + 5 * d + j)

    for j in range(5):
        for d in (0, 1):
            w1_f_in(d, j).wait_recv()
            far_share(yf, c, d, j).start()
    for j in range(5):
        for d in (0, 1):
            far_share(yf, 1 - c, d, j).wait_recv()
    oz_go(3, 2)
    project_prepared(yf)

    @pl.when(main)
    def _():
        own_len.wait()

    @pl.when(jnp.logical_not(main))
    def _():
        remote(len_own, lenb, n_ss.at[0], n_rs.at[0], partner).wait_recv()

    rs = lax.rsqrt(jnp.sum(ssq[...], axis=1, keepdims=True) * (1.0 / 8192.0) + 1e-05)

    def rotate(v):
        return (v * cos[...] + pltpu.roll(v, 64, 1) * sin[...]).astype(jnp.bfloat16)

    rk = rotate(acc[:, 512:640] * rs)
    rv = (acc[:, 640:768] * rs).astype(jnp.bfloat16)
    i_pos = lax.broadcasted_iota(jnp.int32, (SEQ, SEQ), 0)
    j_pos = lax.broadcasted_iota(jnp.int32, (SEQ, SEQ), 1)
    keep = jnp.logical_and(j_pos <= i_pos, j_pos < lenb[0:1, 0:1])
    scale = 1.0 / float(np.sqrt(128.0))
    t_here = 2 * l + h

    def a_self(ld):
        return jnp.logical_and(main, l == ld)

    def a_out(ld, hd):
        return remote(aout.at[hd], ab.at[t_here, hd], a_ss.at[ld, hd], a_rs.at[t_here, hd], device(y, c, z, ld, c))

    def a_in(t, hd):
        return remote(aout.at[hd], ab.at[t, hd], a_ss.at[0, hd], a_rs.at[t, hd], sibling)

    def b_copy(t, hd):
        return remote(ab.at[t, hd], ab.at[t, hd], b_ss.at[t, hd], b_rs.at[t, hd], sibling)

    for hd in range(HEADS):
        rq = rotate(acc[:, hd * HEAD : (hd + 1) * HEAD] * rs)
        s = lax.dot_general(rq, rk, (((1,), (1,)), ((), ())), preferred_element_type=jnp.float32) * scale
        s = jnp.where(keep, s, jnp.float32(-1e30))
        e = jnp.exp(s - jnp.max(s, axis=1, keepdims=True))
        total = jnp.sum(e, axis=1, keepdims=True)
        o = jnp.dot(e.astype(jnp.bfloat16), rv, preferred_element_type=jnp.float32) / total
        o = o.astype(jnp.bfloat16)
        aout[hd] = o
        for ld in (0, 1):
            @pl.when(jnp.logical_not(a_self(ld)))
            def _():
                a_out(ld, hd).start()

        @pl.when(main)
        def _():
            ab[t_here, hd] = o
            b_copy(t_here, hd).start()

    for d in (0, 1):
        g_y_in(d, d).wait_recv()
        g_f(d).start()

    def attended_here(t, hd):
        @pl.when(jnp.logical_and(main, t != t_here))
        def _():
            a_in(t, hd).wait_recv()
            b_copy(t, hd).start()

        @pl.when(jnp.logical_not(main))
        def _():
            b_copy(t, hd).wait_recv()

    def product(zz, groups, heads):
        n = len(heads) * HEAD
        rows_w = pl.ds(heads[0] * HEAD, n)
        a = jnp.concatenate([ab[t, hd] for t in groups for hd in heads], axis=1)
        w = jnp.concatenate(
            [jnp.concatenate([wo[zz, 2 * t, rows_w], wo[zz, 2 * t + 1, rows_w]], axis=1) for t in groups], axis=0
        )
        return jnp.dot(a, w, preferred_element_type=jnp.float32)

    for part in (0, 1):
        heads = (2 * part, 2 * part + 1)
        for hd in heads:
            for t in range(4):
                attended_here(t, hd)

        def out_body(j, _, heads=heads):
            zz = (z + j + NZ - 2) % NZ
            mixed[zz] += product(zz, (0, 1, 2), heads)
            return 0

        lax.fori_loop(0, 5, out_body, 0)
        if part == 0:
            for d in (0, 1):
                for kind in (1, 2):
                    oz_in(3, d, kind).wait_recv()
            far_in.wait_recv()
        lax.fori_loop(5, NZ, out_body, 0)
    for d in (0, 1):
        g_y_in(d, 1 - d).wait_recv()
        g_f_in(d).wait_recv()

    def last_body(zz, _):
        total = mixed[zz] + product(zz, (3,), (0, 1, 2, 3))
        for hh in (0, 1):
            cols = pl.ds(pl.multiple_of(hh * 1024 + zz * 128, 128), 128)
            out[:, cols] = total[:, hh * 128 : (hh + 1) * 128].astype(jnp.bfloat16)
        return 0

    lax.fori_loop(0, NZ, last_body, 0)

    @pl.when(jnp.logical_not(main))
    def _():
        exchange.wait_send()
        len_out.wait_send()
        tok_copy(x, 0, 2).wait_send()
        tok_copy(x, 1, 2).wait_send()

    for hd in (0, 1):
        @pl.when(jnp.logical_not(jnp.logical_and(source, h == hd)))
        def _():
            ox[hd].wait_send()
    for k in (0, 1):
        tok_copy(pair_x, k, 0).wait_send()
        tok_copy(outer_x, k, 1).wait_send()
        tok_forward(k).wait_send()
    for d in (0, 1):
        for i in range(8):
            w1_y(d, i).wait_send()
        for j in range(5):
            w1_f(d, j).wait_send()
            far_share(yf, c, d, j).wait_send()
        for s in (1, 2, 3, 4):
            w1_z(s, d).wait_send()
            g_z(s, d).wait_send()
        for k in (0, 1):
            g_y(d, k).wait_send()
        for s in (1, 2, 3):
            for kind in (0, 1, 2):
                oz(s, d, kind).wait_send()
        oz(4, d, 0).wait_send()
        g_f(d).wait_send()
    far_out.wait_send()
    share(plane(y, c), 0).wait_send()
    share(plane(yn, c), 1).wait_send()
    share(plane(yp, c), 2).wait_send()

    @pl.when(source)
    def _():
        for q in (1, 2, 3):
            scatter(q).wait_send()
        for d in (0, 1):
            for k in (0, 1):
                oy(d, k).wait_send()

    for k in (0, 1):
        @pl.when(jnp.logical_and(rel == 1, c == 1))
        def _():
            oy(0, k).wait_send()

        @pl.when(jnp.logical_and(rel == 3, c == 0))
        def _():
            oy(1, k).wait_send()

    for hd in range(HEADS):
        for ld in (0, 1):
            @pl.when(jnp.logical_not(a_self(ld)))
            def _():
                a_out(ld, hd).wait_send()

        @pl.when(main)
        def _():
            for t in range(4):
                b_copy(t, hd).wait_send()


def per_device(tokens, norm_gain, q_weight, key_value_weight, output_weight, lengths):
    cosine, sine = rotary_tables()
    dma = pltpu.SemaphoreType.DMA
    vmem = pl.BlockSpec(memory_space=pltpu.VMEM)
    bf16 = jnp.bfloat16
    return pl.pallas_call(
        kernel,
        out_shape=jax.ShapeDtypeStruct((SEQ, FEATS), bf16),
        in_specs=[pl.BlockSpec(memory_space=pl.ANY)] + [vmem] * 4 + [pl.BlockSpec(memory_space=pltpu.SMEM)] + [vmem] * 2,
        out_specs=vmem,
        scratch_shapes=[
            pltpu.VMEM((SEQ, FEATS), bf16),
            pltpu.VMEM((1, 4 * FEATS), jnp.float32),
            pltpu.VMEM((128, 768), bf16),
            pltpu.VMEM((8, 128), jnp.int32),
            pltpu.VMEM((4, SEQ, FEATS), bf16),
            pltpu.VMEM((64, 128, 768), bf16),
            pltpu.VMEM((NZ + 1, 8, 512, 128), bf16),
            pltpu.VMEM((4, HEADS, SEQ, HEAD), bf16),
            pltpu.VMEM((HEADS, SEQ, HEAD), bf16),
            pltpu.VMEM((8, 128), jnp.int32),
            pltpu.VMEM((SEQ, 768), jnp.float32),
            pltpu.VMEM((SEQ, 128), jnp.float32),
            pltpu.VMEM((SEQ, FEATS), bf16),
            pltpu.VMEM((NZ, SEQ, 256), jnp.float32),
            dma((3, 2)), dma((4, 2)), dma((2,)), dma((6,)), dma((1,)), dma((1,)), dma((1,)), dma((1,)),
            dma((2, 4)), dma((2, 4)), dma((2, 8)), dma((2, 8)), dma((2, 5)), dma((2, 5)), dma((13,)), dma((13,)),
            dma((2,)), dma((8,)), dma((2, 2)), dma((2,)), dma((2, 4, 3)), dma((2, 4, 3)),
            dma((3,)), dma((1,)), dma((2, 4)), dma((2, 4)), dma((2, 3)), dma((2, 3)), dma((1,)), dma((1,)),
            dma((2, HEADS)), dma((4, HEADS)), dma((4, HEADS)), dma((4, HEADS)),
        ],
        compiler_params=pltpu.CompilerParams(
            collective_id=0, has_side_effects=True, vmem_limit_bytes=56 * 2**20
        ),
        cost_estimate=pl.CostEstimate(flops=8 * 10**9, bytes_accessed=4 * 2**20, transcendentals=600000),
    )(tokens, norm_gain, q_weight, key_value_weight, output_weight, lengths, jnp.asarray(cosine), jnp.asarray(sine))


def solution(mesh):
    return jax.shard_map(
        per_device,
        mesh=mesh,
        in_specs=(
            P("dp", "tensor"),
            P(),
            P("dp", "tensor"),
            P("dp", None, "tensor"),
            P("tensor", "dp"),
            P("dp"),
        ),
        out_specs=P("dp", "tensor"),
        check_vma=False,
    )
```

```python
import functools

import jax
import jax.numpy as jnp
import numpy as np
from jax import lax
from jax.experimental import pallas as pl
from jax.experimental.pallas import tpu as pltpu
from jax.sharding import PartitionSpec as P

MESH = pl.DeviceIdType.MESH
SEQ = 384
HEAD = 128
HEADS = 4
FEATS = 2048
NY, NH, NZ = 4, 2, 8


def rotary_tables():
    half = HEAD // 2
    freqs = 500000.0 ** (-(np.arange(half, dtype=np.float64) * 2.0 / HEAD))
    angles = np.arange(SEQ, dtype=np.float64)[:, None] * freqs[None, :]
    cosine, sine = np.cos(angles), np.sin(angles)
    return (
        np.concatenate([cosine, cosine], axis=1).astype(np.float32),
        np.concatenate([-sine, sine], axis=1).astype(np.float32),
    )


def device(y, h, z, l, c):
    return (y * (NH * NZ) + h * NZ + z, l * 2 + c)


def kernel(
    tok, gain_in, q_own, kv_own, wo_own, length, cos, sin, out,
    tok_own, gain, w1_own, len_own, xb, w1, wo, ab, aout, lenb, acc, ssq, scaled, mixed,
    t_ss, t_rs, t_fs, l_sem, e_ss, e_rs, n_ss, n_rs,
    z_ss, z_rs, y_ss, y_rs, f_ss, f_rs, c_ss, c_rs,
    ox_ss, ox_rs, oy_ss, oy_rs, oz_ss, oz_rs,
    q_ss, q_rs, gz_ss, gz_rs, gy_ss, gy_rs, x2_ss, x2_rs,
    a_ss, a_rs, b_ss, b_rs,
):
    dp = lax.axis_index("dp")
    tensor = lax.axis_index("tensor")
    y, h, z = dp // (NH * NZ), (dp // NZ) % NH, dp % NZ
    l, c = tensor // 2, tensor % 2
    x = 2 * h + l
    main = c == h
    yp, yn = (y + 1) % NY, (y + NY - 1) % NY

    def zat(k):
        return (z + k + NZ) % NZ

    def at_x(xx, cc):
        return device(y, xx // 2, z, xx % 2, cc)

    def remote(src, dst, ss, rs, dev):
        return pltpu.make_async_remote_copy(
            src_ref=src, dst_ref=dst, send_sem=ss, recv_sem=rs, device_id=dev, device_id_type=MESH
        )

    xnext, xprev = (x + 1) % 4, (x + 3) % 4
    sibling = device(y, h, z, l, 1 - c)
    z_dev = (device(y, h, zat(1), l, c), device(y, h, zat(-1), l, c))
    y_dev = (device(yp, h, z, l, c), device(yn, h, z, l, c))

    barrier = pltpu.get_barrier_semaphore()
    partners = [sibling, *z_dev, *y_dev, device((y + 2) % NY, h, z, l, c)]
    for k in (1, 2, 3):
        for cc in (0, 1):
            partners.append(at_x((x + k) % 4, cc))
    for p in partners:
        pl.semaphore_signal(barrier, inc=1, device_id=p, device_id_type=MESH)
    w1_own[:, :512] = q_own[...]
    w1_own[:, 512:640] = kv_own[:, 0, :]
    w1_own[:, 640:] = kv_own[:, 1, :]
    len_own[...] = jnp.full((8, 128), length[0], jnp.int32)
    pl.semaphore_wait(barrier, len(partners))

    me1 = y * 16 + c * 8 + z
    partner = device(y, 1 - h, z, l, 1 - c)
    exchange = remote(w1_own, w1.at[y * 16 + (1 - c) * 8 + z], e_ss.at[0], e_rs.at[0], partner)
    exchange_in = remote(w1_own, w1.at[me1], e_ss.at[0], e_rs.at[0], partner)
    len_out = remote(len_own, lenb, n_ss.at[0], n_rs.at[0], partner)
    own1 = pltpu.make_async_copy(w1_own, w1.at[me1], l_sem.at[0])
    own_len = pltpu.make_async_copy(len_own, lenb, l_sem.at[1])

    @pl.when(main)
    def _():
        own1.start()
        own_len.start()

    @pl.when(jnp.logical_not(main))
    def _():
        exchange.start()
        len_out.start()

    own_t = 2 * l + c
    rel = (y + NY - own_t) % NY
    source = rel == 0
    ox_dev = [device(y, hd, z, y // 2, y % 2) for hd in (0, 1)]
    own_u = wo.at[jnp.where(own_t == 3, NZ, z), 2 * own_t + h]
    ox = [remote(wo_own, own_u, ox_ss.at[hd], ox_rs.at[2 * own_t + h], ox_dev[hd]) for hd in (0, 1)]
    own_o = pltpu.make_async_copy(wo_own, own_u, l_sem.at[2])
    for hd in (0, 1):
        @pl.when(jnp.logical_not(jnp.logical_and(source, h == hd)))
        def _():
            ox[hd].start()

    @pl.when(source)
    def _():
        own_o.start()

    half = SEQ // 2

    def rows(k):
        return pl.ds(k * half, half)

    r = (x + 4 - 2 * c) % 4
    up = jnp.logical_or(r == 1, r == 2)
    fwd_half = jnp.where(r >= 2, 1, 0)

    def tok_copy(dst_x, k, i):
        return remote(tok.at[rows(k)], xb.at[own_t, rows(k)], t_ss.at[i, k], t_rs.at[own_t, k], at_x(dst_x, h))

    pair_x = jnp.where(l == 0, xnext, xprev)
    outer_x = jnp.where(l == 0, xprev, xnext)
    own_tok = pltpu.make_async_copy(tok, xb.at[own_t], l_sem.at[3])
    keep_tok = pltpu.make_async_copy(tok, tok_own, l_sem.at[4])
    tok_copy(pair_x, 0, 0).start()
    tok_copy(outer_x, 1, 1).start()
    tok_copy(pair_x, 1, 0).start()
    tok_copy(outer_x, 0, 1).start()

    @pl.when(main)
    def _():
        own_tok.start()

    @pl.when(jnp.logical_not(main))
    def _():
        tok_copy(x, 0, 2).start()
        tok_copy(x, 1, 2).start()

    def got_tok(f, k):
        return remote(tok.at[rows(k)], xb.at[f, rows(k)], t_ss.at[0, k], t_rs.at[f, k], sibling)

    near_pair = jnp.where(jnp.logical_or(r == 0, r == 2), 1, 0)
    fwd_x = jnp.where(up, xnext, xprev)

    def tok_forward(j):
        f = 2 * near_pair + j
        piece = xb.at[f, pl.ds(pl.multiple_of(fwd_half * half, half), half)]
        return remote(piece, piece, t_fs.at[j], t_rs.at[f, fwd_half], at_x(fwd_x, c))

    def blk(yy, origin):
        return w1.at[yy * 16 + c * 8 + origin]

    def halves(b, d):
        return b.at[pl.ds(64 * d, 64)]

    def ring(cut, piece, ss, rs):
        def at(origin, s, d):
            b = piece(origin)
            return cut(b, d) if s == 4 else b

        def send(s, d):
            b = at(zat(1 - s) if d == 0 else zat(s - 1), s, d)
            return remote(b, b, ss.at[d, s - 1], rs.at[d, s - 1], z_dev[d])

        def take(s, d):
            b = at(zat(-s) if d == 0 else zat(s), s, d)
            return remote(b, b, ss.at[d, s - 1], rs.at[d, s - 1], z_dev[d])

        return send, take

    w1_z, w1_z_in = ring(halves, lambda o: blk(y, o), z_ss, z_rs)

    def slot(i):
        return zat((0, -1, -2, -3, 1, 2, 3, 4)[i])

    def w1_y(d, i):
        b = blk(y, slot(i))
        return remote(b, b, y_ss.at[d, i], y_rs.at[d, i], y_dev[d])

    def w1_y_in(d, i):
        b = blk(yn if d == 0 else yp, slot(i))
        return remote(b, b, y_ss.at[d, i], y_rs.at[d, i], y_dev[d])

    def far_piece(yy, d, j):
        i = (0, 1 + 3 * d, 2 + 3 * d, 3 + 3 * d, 7)[j]
        b = blk(yy, slot(i))
        return halves(b, d) if j in (0, 4) else b

    def w1_f(d, j):
        b = far_piece(yn if d == 0 else yp, d, j)
        return remote(b, b, f_ss.at[d, j], f_rs.at[d, j], y_dev[d])

    yf = (y + 2) % NY

    def w1_f_in(d, j):
        b = far_piece(yf, d, j)
        return remote(b, b, f_ss.at[d, j], f_rs.at[d, j], y_dev[d])

    def share(b, i):
        return remote(b, b, c_ss.at[i], c_rs.at[i], sibling)

    def plane(yy, core):
        return w1.at[pl.ds(yy * 16 + core * 8, 8)]

    def quarter(zz, q):
        return wo.at[zz, 6 + q // 2, pl.ds((q % 2) * 256, 256)]

    def scatter(q):
        return remote(
            quarter(NZ, q), quarter(z, q), q_ss.at[q - 1], q_rs.at[0], device((y + q) % NY, h, z, l, c)
        )

    own_q = pltpu.make_async_copy(quarter(NZ, 0), quarter(z, 0), l_sem.at[5])

    def scatter_in():
        b = quarter(z, rel)
        return remote(b, b, q_ss.at[0], q_rs.at[0], sibling)

    g_z, g_z_in = ring(
        lambda b, d: b.at[pl.ds(128 * d, 128)], lambda o: quarter(o, rel), gz_ss, gz_rs
    )

    def line(yy, k):
        q = (yy + NY - own_t) % NY
        return wo.at[pl.ds(4 * k, 4), 6 + q // 2, pl.ds((q % 2) * 256, 256)]

    def g_y(d, k):
        b = line(y, k)
        return remote(b, b, gy_ss.at[d, k], gy_rs.at[d, k], y_dev[d])

    def g_y_in(d, k):
        b = line(yn if d == 0 else yp, k)
        return remote(b, b, gy_ss.at[d, k], gy_rs.at[d, k], y_dev[d])

    def g_f(d):
        b = line(yn if d == 0 else yp, d)
        return remote(b, b, gy_ss.at[d, 2], gy_rs.at[d, 2], y_dev[d])

    def g_f_in(d):
        b = line(yf, d)
        return remote(b, b, gy_ss.at[d, 2], gy_rs.at[d, 2], y_dev[d])

    def oy(d, k):
        b = wo.at[z, pl.ds(3 * h if k == 0 else 3 - 3 * h, 3)]
        return remote(b, b, oy_ss.at[d, k], oy_rs.at[k], y_dev[d])

    def oz_piece(origin, d, kind):
        if kind == 2:
            return wo.at[origin, pl.ds(3 - 3 * h, 3)]
        return wo.at[origin, pl.ds(3 * h, 3), pl.ds(256 * (d if kind == 0 else 1 - d), 256)]

    def oz(s, d, kind):
        b = oz_piece(zat(1 - s) if d == 0 else zat(s - 1), d, kind)
        return remote(b, b, oz_ss.at[d, s - 1, kind], oz_rs.at[d, s - 1, kind], z_dev[d])

    def oz_in(s, d, kind):
        b = oz_piece(zat(-s) if d == 0 else zat(s), d, kind)
        return remote(b, b, oz_ss.at[d, s - 1, kind], oz_rs.at[d, s - 1, kind], z_dev[d])

    def oz_go(s, kind):
        for d in (0, 1):
            if s > 1:
                oz_in(s - 1, d, kind).wait_recv()
            oz(s, d, kind).start()

    def g_go(s):
        for d in (0, 1):
            if s > 1:
                g_z_in(s - 1, d).wait_recv()
            g_z(s, d).start()

    half_out = wo.at[zat(4), pl.ds(3 * h, 3)]
    half_in = wo.at[zat(4), pl.ds(3 * (1 - h), 3)]
    far_out = remote(half_out, half_out, x2_ss.at[0], x2_rs.at[0], device(y, 1 - h, z, l, c))
    far_in = remote(half_in, half_in, x2_ss.at[0], x2_rs.at[0], device(y, 1 - h, z, l, c))

    @pl.when(main)
    def _():
        own1.wait()

    @pl.when(jnp.logical_not(main))
    def _():
        exchange_in.wait_recv()

    for d in (0, 1):
        w1_z(1, d).start()

    @pl.when(source)
    def _():
        own_o.wait()
        for u in range(8):
            @pl.when(u != 2 * own_t + h)
            def _():
                remote(wo_own, wo.at[z if u < 6 else NZ, u], ox_ss.at[0], ox_rs.at[u], sibling).wait_recv()
        own_q.start()
        for q in (1, 3, 2):
            scatter(q).start()
        for k in (0, 1):
            for d in (0, 1):
                oy(d, k).start()

    later = (jnp.logical_and(rel == 1, c == 1), jnp.logical_and(rel == 3, c == 0))

    def y_start(group, *ways):
        for d in (0, 1):
            @pl.when(ways[d])
            def _():
                for i in group:
                    w1_y(d, i).start()

    at_once = tuple(jnp.logical_not(v) for v in later)
    y_start((0,), *at_once)
    for s in (2, 3, 4):
        for d in (0, 1):
            w1_z_in(s - 1, d).wait_recv()
            w1_z(s, d).start()
        if s < 4:
            k = s - 2

            @pl.when(jnp.logical_or(rel == 1, rel == 3))
            def _():
                oy(0, k).wait_recv()

            for d in (0, 1):
                @pl.when(later[d])
                def _():
                    oy(d, k).start()

        if s == 2:
            y_start((1, 4), *at_once)
        if s == 3:
            y_start((0, 1, 4), *later)

            @pl.when(jnp.logical_not(source))
            def _():
                scatter_in().wait_recv()

            @pl.when(source)
            def _():
                own_q.wait()

            g_go(1)

    g_go(2)
    for i in (2, 5, 3, 6):
        for d in (0, 1):
            w1_y(d, i).start()

    for d in (0, 1):
        w1_z_in(4, d).wait_recv()
    for d in (0, 1):
        w1_y(d, 7).start()
    share(plane(y, c), 0).start()
    g_go(3)

    @pl.when(rel == 2)
    def _():
        oy(0, 0).wait_recv()

    oz_go(1, 0)
    oz_go(1, 1)


    def y_group(group, j):
        for d in (0, 1):
            for i in group:
                w1_y_in(d, i).wait_recv()
            w1_f(d, j).start()

    for j in (0, 1):
        got_tok(2 * near_pair + j, fwd_half).wait_recv()
        tok_forward(j).start()
    g_go(4)
    y_group((0,), 0)
    oz_go(2, 0)

    @pl.when(rel == 2)
    def _():
        oy(0, 1).wait_recv()

    oz_go(1, 2)
    y_group((1, 4), 1)
    oz_go(3, 0)
    oz_go(2, 1)
    y_group((2, 5), 2)
    y_group((3, 6), 3)
    oz_go(4, 0)
    oz_go(2, 2)
    y_group((7,), 4)
    share(plane(yn, c), 1).start()
    share(plane(yp, c), 2).start()
    for d in (0, 1):
        g_z_in(4, d).wait_recv()
    for d in (0, 1):
        for k in (0, 1):
            g_y(d, k if d == 0 else 1 - k).start()
    gain[...] = gain_in[...].astype(jnp.float32).reshape(1, 4 * FEATS)
    acc[...] = jnp.zeros_like(acc)
    ssq[...] = jnp.zeros_like(ssq)

    def project(f):
        def body(i, _):
            cols = pl.ds(pl.multiple_of(i * 512, 512), 512)
            xf = xb[f, :, cols].astype(jnp.float32)
            sq = xf * xf
            ssq[...] += sq[:, :128] + sq[:, 128:256] + sq[:, 256:384] + sq[:, 384:]
            g = gain[:, pl.ds(pl.multiple_of(f * FEATS + i * 512, 512), 512)]
            xg = (xf * g).astype(jnp.bfloat16)
            w = w1[pl.ds(f * 16 + i * 4, 4)].reshape(512, 768)
            acc[...] += jnp.dot(xg, w, preferred_element_type=jnp.float32)
            return 0

        lax.fori_loop(0, 4, body, 0)

    def prepare(f):
        def body(i, _):
            cols = pl.ds(pl.multiple_of(i * 512, 512), 512)
            xf = xb[f, :, cols].astype(jnp.float32)
            sq = xf * xf
            ssq[...] += sq[:, :128] + sq[:, 128:256] + sq[:, 256:384] + sq[:, 384:]
            g = gain[:, pl.ds(pl.multiple_of(f * FEATS + i * 512, 512), 512)]
            scaled[:, cols] = (xf * g).astype(jnp.bfloat16)
            return 0

        lax.fori_loop(0, 4, body, 0)

    def project_prepared(f):
        def body(i, _):
            cols = pl.ds(pl.multiple_of(i * 512, 512), 512)
            w = w1[pl.ds(f * 16 + i * 4, 4)].reshape(512, 768)
            acc[...] += jnp.dot(scaled[:, cols], w, preferred_element_type=jnp.float32)
            return 0

        lax.fori_loop(0, 4, body, 0)

    keep_tok.start()

    def tokens_here(f):
        own = jnp.logical_and(main, f == own_t)

        @pl.when(own)
        def _():
            own_tok.wait()

        for k in (0, 1):
            handed = jnp.logical_and(f // 2 == near_pair, k == fwd_half)

            @pl.when(jnp.logical_not(jnp.logical_or(own, handed)))
            def _():
                got_tok(f, k).wait_recv()

    share(plane(y, 1 - c), 0).wait_recv()
    tokens_here(y)
    project(y)
    oz_go(3, 1)
    share(plane(yn, 1 - c), 1).wait_recv()
    tokens_here(yn)
    project(yn)
    for d in (0, 1):
        oz_in(4, d, 0).wait_recv()
    far_out.start()
    share(plane(yp, 1 - c), 2).wait_recv()
    tokens_here(yp)
    project(yp)
    tokens_here(yf)
    prepare(yf)

    def start_out(zz, _):
        for hh in (0, 1):
            cols = pl.ds(pl.multiple_of(hh * 1024 + zz * 128, 128), 128)
            mixed[zz, :, hh * 128 : (hh + 1) * 128] = tok_own[:, cols].astype(jnp.float32)
        return 0

    keep_tok.wait()
    lax.fori_loop(0, NZ, start_out, 0)

    def far_share(yy, core, d, j):
        i = (0, 1 + 3 * d, 2 + 3 * d, 3 + 3 * d, 7)[j]
        b = w1.at[yy * 16 + core * 8 + slot(i)]
        return share(halves(b, d) if j in (0, 4) else b, 3 + 5 * d + j)

    for j in range(5):
        for d in (0, 1):
            w1_f_in(d, j).wait_recv()
            far_share(yf, c, d, j).start()
    for j in range(5):
        for d in (0, 1):
            far_share(yf, 1 - c, d, j).wait_recv()
    oz_go(3, 2)
    project_prepared(yf)

    @pl.when(main)
    def _():
        own_len.wait()

    @pl.when(jnp.logical_not(main))
    def _():
        remote(len_own, lenb, n_ss.at[0], n_rs.at[0], partner).wait_recv()

    rs = lax.rsqrt(jnp.sum(ssq[...], axis=1, keepdims=True) * (1.0 / 8192.0) + 1e-05)

    def rotate(v):
        return (v * cos[...] + pltpu.roll(v, 64, 1) * sin[...]).astype(jnp.bfloat16)

    rk = rotate(acc[:, 512:640] * rs)
    rv = (acc[:, 640:768] * rs).astype(jnp.bfloat16)
    i_pos = lax.broadcasted_iota(jnp.int32, (SEQ, SEQ), 0)
    j_pos = lax.broadcasted_iota(jnp.int32, (SEQ, SEQ), 1)
    keep = jnp.logical_and(j_pos <= i_pos, j_pos < lenb[0:1, 0:1])
    scale = 1.0 / float(np.sqrt(128.0))
    t_here = 2 * l + h

    def a_self(ld):
        return jnp.logical_and(main, l == ld)

    def a_out(ld, hd):
        return remote(aout.at[hd], ab.at[t_here, hd], a_ss.at[ld, hd], a_rs.at[t_here, hd], device(y, c, z, ld, c))

    def a_in(t, hd):
        return remote(aout.at[hd], ab.at[t, hd], a_ss.at[0, hd], a_rs.at[t, hd], sibling)

    def b_copy(t, hd):
        return remote(ab.at[t, hd], ab.at[t, hd], b_ss.at[t, hd], b_rs.at[t, hd], sibling)

    for hd in range(HEADS):
        rq = rotate(acc[:, hd * HEAD : (hd + 1) * HEAD] * rs)
        s = lax.dot_general(rq, rk, (((1,), (1,)), ((), ())), preferred_element_type=jnp.float32) * scale
        s = jnp.where(keep, s, jnp.float32(-1e30))
        e = jnp.exp(s - jnp.max(s, axis=1, keepdims=True))
        total = jnp.sum(e, axis=1, keepdims=True)
        o = jnp.dot(e.astype(jnp.bfloat16), rv, preferred_element_type=jnp.float32) / total
        o = o.astype(jnp.bfloat16)
        aout[hd] = o
        for ld in (0, 1):
            @pl.when(jnp.logical_not(a_self(ld)))
            def _():
                a_out(ld, hd).start()

        @pl.when(main)
        def _():
            ab[t_here, hd] = o
            b_copy(t_here, hd).start()

    for d in (0, 1):
        g_y_in(d, d).wait_recv()
        g_f(d).start()

    def attended_here(t, hd):
        @pl.when(jnp.logical_and(main, t != t_here))
        def _():
            a_in(t, hd).wait_recv()
            b_copy(t, hd).start()

        @pl.when(jnp.logical_not(main))
        def _():
            b_copy(t, hd).wait_recv()

    def product(zz, groups, heads):
        n = len(heads) * HEAD
        rows_w = pl.ds(heads[0] * HEAD, n)
        a = jnp.concatenate([ab[t, hd] for t in groups for hd in heads], axis=1)
        w = jnp.concatenate(
            [jnp.concatenate([wo[zz, 2 * t, rows_w], wo[zz, 2 * t + 1, rows_w]], axis=1) for t in groups], axis=0
        )
        return jnp.dot(a, w, preferred_element_type=jnp.float32)

    for part in (0, 1):
        heads = (2 * part, 2 * part + 1)
        for hd in heads:
            for t in range(4):
                attended_here(t, hd)

        def out_body(j, _, heads=heads):
            zz = (z + j + NZ - 2) % NZ
            mixed[zz] += product(zz, (0, 1, 2), heads)
            return 0

        lax.fori_loop(0, 5, out_body, 0)
        if part == 0:
            for d in (0, 1):
                for kind in (1, 2):
                    oz_in(3, d, kind).wait_recv()
            far_in.wait_recv()
        lax.fori_loop(5, NZ, out_body, 0)
    for d in (0, 1):
        g_y_in(d, 1 - d).wait_recv()
        g_f_in(d).wait_recv()

    def last_body(zz, _):
        total = mixed[zz] + product(zz, (3,), (0, 1, 2, 3))
        for hh in (0, 1):
            cols = pl.ds(pl.multiple_of(hh * 1024 + zz * 128, 128), 128)
            out[:, cols] = total[:, hh * 128 : (hh + 1) * 128].astype(jnp.bfloat16)
        return 0

    lax.fori_loop(0, NZ, last_body, 0)

    @pl.when(jnp.logical_not(main))
    def _():
        exchange.wait_send()
        len_out.wait_send()
        tok_copy(x, 0, 2).wait_send()
        tok_copy(x, 1, 2).wait_send()

    for hd in (0, 1):
        @pl.when(jnp.logical_not(jnp.logical_and(source, h == hd)))
        def _():
            ox[hd].wait_send()
    for k in (0, 1):
        tok_copy(pair_x, k, 0).wait_send()
        tok_copy(outer_x, k, 1).wait_send()
        tok_forward(k).wait_send()
    for d in (0, 1):
        for i in range(8):
            w1_y(d, i).wait_send()
        for j in range(5):
            w1_f(d, j).wait_send()
            far_share(yf, c, d, j).wait_send()
        for s in (1, 2, 3, 4):
            w1_z(s, d).wait_send()
            g_z(s, d).wait_send()
        for k in (0, 1):
            g_y(d, k).wait_send()
        for s in (1, 2, 3):
            for kind in (0, 1, 2):
                oz(s, d, kind).wait_send()
        oz(4, d, 0).wait_send()
        g_f(d).wait_send()
    far_out.wait_send()
    share(plane(y, c), 0).wait_send()
    share(plane(yn, c), 1).wait_send()
    share(plane(yp, c), 2).wait_send()

    @pl.when(source)
    def _():
        for q in (1, 2, 3):
            scatter(q).wait_send()
        for d in (0, 1):
            for k in (0, 1):
                oy(d, k).wait_send()

    for k in (0, 1):
        @pl.when(jnp.logical_and(rel == 1, c == 1))
        def _():
            oy(0, k).wait_send()

        @pl.when(jnp.logical_and(rel == 3, c == 0))
        def _():
            oy(1, k).wait_send()

    for hd in range(HEADS):
        for ld in (0, 1):
            @pl.when(jnp.logical_not(a_self(ld)))
            def _():
                a_out(ld, hd).wait_send()

        @pl.when(main)
        def _():
            for t in range(4):
                b_copy(t, hd).wait_send()


def per_device(tokens, norm_gain, q_weight, key_value_weight, output_weight, lengths):
    cosine, sine = rotary_tables()
    dma = pltpu.SemaphoreType.DMA
    vmem = pl.BlockSpec(memory_space=pltpu.VMEM)
    bf16 = jnp.bfloat16
    return pl.pallas_call(
        kernel,
        out_shape=pltpu.VMEM((SEQ, FEATS), bf16),
        in_specs=[pl.BlockSpec(memory_space=pl.ANY)] + [vmem] * 4 + [pl.BlockSpec(memory_space=pltpu.SMEM)] + [vmem] * 2,
        out_specs=vmem,
        scratch_shapes=[
            pltpu.VMEM((SEQ, FEATS), bf16),
            pltpu.VMEM((1, 4 * FEATS), jnp.float32),
            pltpu.VMEM((128, 768), bf16),
            pltpu.VMEM((8, 128), jnp.int32),
            pltpu.VMEM((4, SEQ, FEATS), bf16),
            pltpu.VMEM((64, 128, 768), bf16),
            pltpu.VMEM((NZ + 1, 8, 512, 128), bf16),
            pltpu.VMEM((4, HEADS, SEQ, HEAD), bf16),
            pltpu.VMEM((HEADS, SEQ, HEAD), bf16),
            pltpu.VMEM((8, 128), jnp.int32),
            pltpu.VMEM((SEQ, 768), jnp.float32),
            pltpu.VMEM((SEQ, 128), jnp.float32),
            pltpu.VMEM((SEQ, FEATS), bf16),
            pltpu.VMEM((NZ, SEQ, 256), jnp.float32),
            dma((3, 2)), dma((4, 2)), dma((2,)), dma((6,)), dma((1,)), dma((1,)), dma((1,)), dma((1,)),
            dma((2, 4)), dma((2, 4)), dma((2, 8)), dma((2, 8)), dma((2, 5)), dma((2, 5)), dma((13,)), dma((13,)),
            dma((2,)), dma((8,)), dma((2, 2)), dma((2,)), dma((2, 4, 3)), dma((2, 4, 3)),
            dma((3,)), dma((1,)), dma((2, 4)), dma((2, 4)), dma((2, 3)), dma((2, 3)), dma((1,)), dma((1,)),
            dma((2, HEADS)), dma((4, HEADS)), dma((4, HEADS)), dma((4, HEADS)),
        ],
        compiler_params=pltpu.CompilerParams(
            collective_id=0, has_side_effects=True, vmem_limit_bytes=56 * 2**20
        ),
        cost_estimate=pl.CostEstimate(flops=8 * 10**9, bytes_accessed=4 * 2**20, transcendentals=600000),
    )(tokens, norm_gain, q_weight, key_value_weight, output_weight, lengths, jnp.asarray(cosine), jnp.asarray(sine))


def solution(mesh):
    return jax.shard_map(
        per_device,
        mesh=mesh,
        in_specs=(
            P("dp", "tensor"),
            P(),
            P("dp", "tensor"),
            P("dp", None, "tensor"),
            P("tensor", "dp"),
            P("dp"),
        ),
        out_specs=P("dp", "tensor"),
        check_vma=False,
    )
```

```python
import functools

import jax
import jax.numpy as jnp
import numpy as np
from jax import lax
from jax.experimental import pallas as pl
from jax.experimental.pallas import tpu as pltpu
from jax.sharding import PartitionSpec as P

MESH = pl.DeviceIdType.MESH
SEQ = 384
HEAD = 128
HEADS = 4
FEATS = 2048
NY, NH, NZ = 4, 2, 8


def rotary_tables():
    half = HEAD // 2
    freqs = 500000.0 ** (-(np.arange(half, dtype=np.float64) * 2.0 / HEAD))
    angles = np.arange(SEQ, dtype=np.float64)[:, None] * freqs[None, :]
    cosine, sine = np.cos(angles), np.sin(angles)
    return (
        np.concatenate([cosine, cosine], axis=1).astype(np.float32),
        np.concatenate([-sine, sine], axis=1).astype(np.float32),
    )


def device(y, h, z, l, c):
    return (y * (NH * NZ) + h * NZ + z, l * 2 + c)


def kernel(
    tok, gain_in, q_own, kv_own, wo_own, length, cos, sin, out,
    tok_own, gain, w1_own, len_own, xb, w1, wo, ab, aout, lenb, acc, ssq, scaled, mixed,
    t_ss, t_rs, t_fs, l_sem, e_ss, e_rs, n_ss, n_rs,
    z_ss, z_rs, y_ss, y_rs, f_ss, f_rs, c_ss, c_rs,
    ox_ss, ox_rs, oy_ss, oy_rs, oz_ss, oz_rs,
    q_ss, q_rs, gz_ss, gz_rs, gy_ss, gy_rs, x2_ss, x2_rs,
    a_ss, a_rs, b_ss, b_rs,
):
    dp = lax.axis_index("dp")
    tensor = lax.axis_index("tensor")
    y, h, z = dp // (NH * NZ), (dp // NZ) % NH, dp % NZ
    l, c = tensor // 2, tensor % 2
    x = 2 * h + l
    main = c == h
    yp, yn = (y + 1) % NY, (y + NY - 1) % NY

    def zat(k):
        return (z + k + NZ) % NZ

    def at_x(xx, cc):
        return device(y, xx // 2, z, xx % 2, cc)

    def remote(src, dst, ss, rs, dev):
        return pltpu.make_async_remote_copy(
            src_ref=src, dst_ref=dst, send_sem=ss, recv_sem=rs, device_id=dev, device_id_type=MESH
        )

    xnext, xprev = (x + 1) % 4, (x + 3) % 4
    sibling = device(y, h, z, l, 1 - c)
    z_dev = (device(y, h, zat(1), l, c), device(y, h, zat(-1), l, c))
    y_dev = (device(yp, h, z, l, c), device(yn, h, z, l, c))

    barrier = pltpu.get_barrier_semaphore()
    partners = [sibling, *z_dev, *y_dev, device((y + 2) % NY, h, z, l, c)]
    for k in (1, 2, 3):
        for cc in (0, 1):
            partners.append(at_x((x + k) % 4, cc))
    for p in partners:
        pl.semaphore_signal(barrier, inc=1, device_id=p, device_id_type=MESH)
    w1_own[:, :512] = q_own[...]
    w1_own[:, 512:640] = kv_own[:, 0, :]
    w1_own[:, 640:] = kv_own[:, 1, :]
    len_own[...] = jnp.full((8, 128), length[0], jnp.int32)
    pl.semaphore_wait(barrier, len(partners))

    me1 = y * 16 + c * 8 + z
    partner = device(y, 1 - h, z, l, 1 - c)
    exchange = remote(w1_own, w1.at[y * 16 + (1 - c) * 8 + z], e_ss.at[0], e_rs.at[0], partner)
    exchange_in = remote(w1_own, w1.at[me1], e_ss.at[0], e_rs.at[0], partner)
    len_out = remote(len_own, lenb, n_ss.at[0], n_rs.at[0], partner)
    own1 = pltpu.make_async_copy(w1_own, w1.at[me1], l_sem.at[0])
    own_len = pltpu.make_async_copy(len_own, lenb, l_sem.at[1])

    @pl.when(main)
    def _():
        own1.start()
        own_len.start()

    @pl.when(jnp.logical_not(main))
    def _():
        exchange.start()
        len_out.start()

    own_t = 2 * l + c
    rel = (y + NY - own_t) % NY
    source = rel == 0
    ox_dev = [device(y, hd, z, y // 2, y % 2) for hd in (0, 1)]
    own_u = wo.at[jnp.where(own_t == 3, NZ, z), 2 * own_t + h]
    ox = [remote(wo_own, own_u, ox_ss.at[hd], ox_rs.at[2 * own_t + h], ox_dev[hd]) for hd in (0, 1)]
    own_o = pltpu.make_async_copy(wo_own, own_u, l_sem.at[2])
    for hd in (0, 1):
        @pl.when(jnp.logical_not(jnp.logical_and(source, h == hd)))
        def _():
            ox[hd].start()

    @pl.when(source)
    def _():
        own_o.start()

    half = SEQ // 2

    def rows(k):
        return pl.ds(k * half, half)

    r = (x + 4 - 2 * c) % 4
    up = jnp.logical_or(r == 1, r == 2)
    fwd_half = jnp.where(r >= 2, 1, 0)

    def tok_copy(dst_x, k, i):
        return remote(tok.at[rows(k)], xb.at[own_t, rows(k)], t_ss.at[i, k], t_rs.at[own_t, k], at_x(dst_x, h))

    pair_x = jnp.where(l == 0, xnext, xprev)
    outer_x = jnp.where(l == 0, xprev, xnext)
    own_tok = pltpu.make_async_copy(tok, xb.at[own_t], l_sem.at[3])
    keep_tok = pltpu.make_async_copy(tok, tok_own, l_sem.at[4])
    tok_copy(pair_x, 0, 0).start()
    tok_copy(outer_x, 1, 1).start()
    tok_copy(pair_x, 1, 0).start()
    tok_copy(outer_x, 0, 1).start()

    @pl.when(main)
    def _():
        own_tok.start()

    @pl.when(jnp.logical_not(main))
    def _():
        tok_copy(x, 0, 2).start()
        tok_copy(x, 1, 2).start()

    def got_tok(f, k):
        return remote(tok.at[rows(k)], xb.at[f, rows(k)], t_ss.at[0, k], t_rs.at[f, k], sibling)

    near_pair = jnp.where(jnp.logical_or(r == 0, r == 2), 1, 0)
    fwd_x = jnp.where(up, xnext, xprev)

    def tok_forward(j):
        f = 2 * near_pair + j
        piece = xb.at[f, pl.ds(pl.multiple_of(fwd_half * half, half), half)]
        return remote(piece, piece, t_fs.at[j], t_rs.at[f, fwd_half], at_x(fwd_x, c))

    def blk(yy, origin):
        return w1.at[yy * 16 + c * 8 + origin]

    def halves(b, d):
        return b.at[pl.ds(64 * d, 64)]

    def ring(cut, piece, ss, rs):
        def at(origin, s, d):
            b = piece(origin)
            return cut(b, d) if s == 4 else b

        def send(s, d):
            b = at(zat(1 - s) if d == 0 else zat(s - 1), s, d)
            return remote(b, b, ss.at[d, s - 1], rs.at[d, s - 1], z_dev[d])

        def take(s, d):
            b = at(zat(-s) if d == 0 else zat(s), s, d)
            return remote(b, b, ss.at[d, s - 1], rs.at[d, s - 1], z_dev[d])

        return send, take

    w1_z, w1_z_in = ring(halves, lambda o: blk(y, o), z_ss, z_rs)

    def slot(i):
        return zat((0, -1, -2, -3, 1, 2, 3, 4)[i])

    def w1_y(d, i):
        b = blk(y, slot(i))
        return remote(b, b, y_ss.at[d, i], y_rs.at[d, i], y_dev[d])

    def w1_y_in(d, i):
        b = blk(yn if d == 0 else yp, slot(i))
        return remote(b, b, y_ss.at[d, i], y_rs.at[d, i], y_dev[d])

    def far_piece(yy, d, j):
        i = (0, 1 + 3 * d, 2 + 3 * d, 3 + 3 * d, 7)[j]
        b = blk(yy, slot(i))
        return halves(b, d) if j in (0, 4) else b

    def w1_f(d, j):
        b = far_piece(yn if d == 0 else yp, d, j)
        return remote(b, b, f_ss.at[d, j], f_rs.at[d, j], y_dev[d])

    yf = (y + 2) % NY

    def w1_f_in(d, j):
        b = far_piece(yf, d, j)
        return remote(b, b, f_ss.at[d, j], f_rs.at[d, j], y_dev[d])

    def share(b, i):
        return remote(b, b, c_ss.at[i], c_rs.at[i], sibling)

    def plane(yy, core):
        return w1.at[pl.ds(yy * 16 + core * 8, 8)]

    def quarter(zz, q):
        return wo.at[zz, 6 + q // 2, pl.ds((q % 2) * 256, 256)]

    def scatter(q):
        return remote(
            quarter(NZ, q), quarter(z, q), q_ss.at[q - 1], q_rs.at[0], device((y + q) % NY, h, z, l, c)
        )

    own_q = pltpu.make_async_copy(quarter(NZ, 0), quarter(z, 0), l_sem.at[5])

    def scatter_in():
        b = quarter(z, rel)
        return remote(b, b, q_ss.at[0], q_rs.at[0], sibling)

    g_z, g_z_in = ring(
        lambda b, d: b.at[pl.ds(128 * d, 128)], lambda o: quarter(o, rel), gz_ss, gz_rs
    )

    def line(yy, k):
        q = (yy + NY - own_t) % NY
        return wo.at[pl.ds(4 * k, 4), 6 + q // 2, pl.ds((q % 2) * 256, 256)]

    def g_y(d, k):
        b = line(y, k)
        return remote(b, b, gy_ss.at[d, k], gy_rs.at[d, k], y_dev[d])

    def g_y_in(d, k):
        b = line(yn if d == 0 else yp, k)
        return remote(b, b, gy_ss.at[d, k], gy_rs.at[d, k], y_dev[d])

    def g_f(d):
        b = line(yn if d == 0 else yp, d)
        return remote(b, b, gy_ss.at[d, 2], gy_rs.at[d, 2], y_dev[d])

    def g_f_in(d):
        b = line(yf, d)
        return remote(b, b, gy_ss.at[d, 2], gy_rs.at[d, 2], y_dev[d])

    def oy(d, k):
        b = wo.at[z, pl.ds(3 * h if k == 0 else 3 - 3 * h, 3)]
        return remote(b, b, oy_ss.at[d, k], oy_rs.at[k], y_dev[d])

    def oz_piece(origin, d, kind):
        if kind == 2:
            return wo.at[origin, pl.ds(3 - 3 * h, 3)]
        return wo.at[origin, pl.ds(3 * h, 3), pl.ds(256 * (d if kind == 0 else 1 - d), 256)]

    def oz(s, d, kind):
        b = oz_piece(zat(1 - s) if d == 0 else zat(s - 1), d, kind)
        return remote(b, b, oz_ss.at[d, s - 1, kind], oz_rs.at[d, s - 1, kind], z_dev[d])

    def oz_in(s, d, kind):
        b = oz_piece(zat(-s) if d == 0 else zat(s), d, kind)
        return remote(b, b, oz_ss.at[d, s - 1, kind], oz_rs.at[d, s - 1, kind], z_dev[d])

    def oz_go(s, kind):
        for d in (0, 1):
            if s > 1:
                oz_in(s - 1, d, kind).wait_recv()
            oz(s, d, kind).start()

    def g_go(s):
        for d in (0, 1):
            if s > 1:
                g_z_in(s - 1, d).wait_recv()
            g_z(s, d).start()

    half_out = wo.at[zat(4), pl.ds(3 * h, 3)]
    half_in = wo.at[zat(4), pl.ds(3 * (1 - h), 3)]
    far_out = remote(half_out, half_out, x2_ss.at[0], x2_rs.at[0], device(y, 1 - h, z, l, c))
    far_in = remote(half_in, half_in, x2_ss.at[0], x2_rs.at[0], device(y, 1 - h, z, l, c))

    @pl.when(main)
    def _():
        own1.wait()

    @pl.when(jnp.logical_not(main))
    def _():
        exchange_in.wait_recv()

    for d in (0, 1):
        w1_z(1, d).start()

    @pl.when(source)
    def _():
        own_o.wait()
        for u in range(8):
            @pl.when(u != 2 * own_t + h)
            def _():
                remote(wo_own, wo.at[z if u < 6 else NZ, u], ox_ss.at[0], ox_rs.at[u], sibling).wait_recv()
        own_q.start()
        for q in (1, 3, 2):
            scatter(q).start()
        for k in (0, 1):
            for d in (0, 1):
                oy(d, k).start()

    later = (jnp.logical_and(rel == 1, c == 1), jnp.logical_and(rel == 3, c == 0))

    def y_start(group, *ways):
        for d in (0, 1):
            @pl.when(ways[d])
            def _():
                for i in group:
                    w1_y(d, i).start()

    at_once = tuple(jnp.logical_not(v) for v in later)
    y_start((0,), *at_once)
    for s in (2, 3, 4):
        for d in (0, 1):
            w1_z_in(s - 1, d).wait_recv()
            w1_z(s, d).start()
        if s < 4:
            k = s - 2

            @pl.when(jnp.logical_or(rel == 1, rel == 3))
            def _():
                oy(0, k).wait_recv()

            for d in (0, 1):
                @pl.when(later[d])
                def _():
                    oy(d, k).start()

        if s == 2:
            y_start((1, 4), *at_once)
        if s == 3:
            y_start((0, 1, 4), *later)

            @pl.when(jnp.logical_not(source))
            def _():
                scatter_in().wait_recv()

            @pl.when(source)
            def _():
                own_q.wait()

            g_go(1)

    g_go(2)
    for i in (2, 5, 3, 6):
        for d in (0, 1):
            w1_y(d, i).start()

    for d in (0, 1):
        w1_z_in(4, d).wait_recv()
    for d in (0, 1):
        w1_y(d, 7).start()
    share(plane(y, c), 0).start()
    g_go(3)

    @pl.when(rel == 2)
    def _():
        oy(0, 0).wait_recv()

    oz_go(1, 0)
    oz_go(1, 1)


    def y_group(group, j):
        for d in (0, 1):
            for i in group:
                w1_y_in(d, i).wait_recv()
            w1_f(d, j).start()

    g_go(4)
    oz_go(2, 0)
    y_group((0,), 0)
    for j in (0, 1):
        got_tok(2 * near_pair + j, fwd_half).wait_recv()
        tok_forward(j).start()

    @pl.when(rel == 2)
    def _():
        oy(0, 1).wait_recv()

    oz_go(1, 2)
    y_group((1, 4), 1)
    oz_go(3, 0)
    oz_go(2, 1)
    y_group((2, 5), 2)
    y_group((3, 6), 3)
    oz_go(4, 0)
    oz_go(2, 2)
    y_group((7,), 4)
    share(plane(yn, c), 1).start()
    share(plane(yp, c), 2).start()
    for d in (0, 1):
        g_z_in(4, d).wait_recv()
    for d in (0, 1):
        for k in (0, 1):
            g_y(d, k if d == 0 else 1 - k).start()
    gain[...] = gain_in[...].astype(jnp.float32).reshape(1, 4 * FEATS)
    acc[...] = jnp.zeros_like(acc)
    ssq[...] = jnp.zeros_like(ssq)

    def project(f):
        def body(i, _):
            cols = pl.ds(pl.multiple_of(i * 512, 512), 512)
            xf = xb[f, :, cols].astype(jnp.float32)
            sq = xf * xf
            ssq[...] += sq[:, :128] + sq[:, 128:256] + sq[:, 256:384] + sq[:, 384:]
            g = gain[:, pl.ds(pl.multiple_of(f * FEATS + i * 512, 512), 512)]
            xg = (xf * g).astype(jnp.bfloat16)
            w = w1[pl.ds(f * 16 + i * 4, 4)].reshape(512, 768)
            acc[...] += jnp.dot(xg, w, preferred_element_type=jnp.float32)
            return 0

        lax.fori_loop(0, 4, body, 0)

    def prepare(f):
        def body(i, _):
            cols = pl.ds(pl.multiple_of(i * 512, 512), 512)
            xf = xb[f, :, cols].astype(jnp.float32)
            sq = xf * xf
            ssq[...] += sq[:, :128] + sq[:, 128:256] + sq[:, 256:384] + sq[:, 384:]
            g = gain[:, pl.ds(pl.multiple_of(f * FEATS + i * 512, 512), 512)]
            scaled[:, cols] = (xf * g).astype(jnp.bfloat16)
            return 0

        lax.fori_loop(0, 4, body, 0)

    def project_prepared(f):
        def body(i, _):
            cols = pl.ds(pl.multiple_of(i * 512, 512), 512)
            w = w1[pl.ds(f * 16 + i * 4, 4)].reshape(512, 768)
            acc[...] += jnp.dot(scaled[:, cols], w, preferred_element_type=jnp.float32)
            return 0

        lax.fori_loop(0, 4, body, 0)

    keep_tok.start()

    def tokens_here(f):
        own = jnp.logical_and(main, f == own_t)

        @pl.when(own)
        def _():
            own_tok.wait()

        for k in (0, 1):
            handed = jnp.logical_and(f // 2 == near_pair, k == fwd_half)

            @pl.when(jnp.logical_not(jnp.logical_or(own, handed)))
            def _():
                got_tok(f, k).wait_recv()

    share(plane(y, 1 - c), 0).wait_recv()
    tokens_here(y)
    project(y)
    oz_go(3, 1)
    share(plane(yn, 1 - c), 1).wait_recv()
    tokens_here(yn)
    project(yn)
    for d in (0, 1):
        oz_in(4, d, 0).wait_recv()
    far_out.start()
    share(plane(yp, 1 - c), 2).wait_recv()
    tokens_here(yp)
    project(yp)
    tokens_here(yf)
    prepare(yf)

    def start_out(zz, _):
        for hh in (0, 1):
            cols = pl.ds(pl.multiple_of(hh * 1024 + zz * 128, 128), 128)
            mixed[zz, :, hh * 128 : (hh + 1) * 128] = tok_own[:, cols].astype(jnp.float32)
        return 0

    keep_tok.wait()
    lax.fori_loop(0, NZ, start_out, 0)

    def far_share(yy, core, d, j):
        i = (0, 1 + 3 * d, 2 + 3 * d, 3 + 3 * d, 7)[j]
        b = w1.at[yy * 16 + core * 8 + slot(i)]
        return share(halves(b, d) if j in (0, 4) else b, 3 + 5 * d + j)

    for j in range(5):
        for d in (0, 1):
            w1_f_in(d, j).wait_recv()
            far_share(yf, c, d, j).start()
    for j in range(5):
        for d in (0, 1):
            far_share(yf, 1 - c, d, j).wait_recv()
    oz_go(3, 2)
    project_prepared(yf)

    @pl.when(main)
    def _():
        own_len.wait()

    @pl.when(jnp.logical_not(main))
    def _():
        remote(len_own, lenb, n_ss.at[0], n_rs.at[0], partner).wait_recv()

    rs = lax.rsqrt(jnp.sum(ssq[...], axis=1, keepdims=True) * (1.0 / 8192.0) + 1e-05)

    def rotate(v):
        return (v * cos[...] + pltpu.roll(v, 64, 1) * sin[...]).astype(jnp.bfloat16)

    rk = rotate(acc[:, 512:640] * rs)
    rv = (acc[:, 640:768] * rs).astype(jnp.bfloat16)
    i_pos = lax.broadcasted_iota(jnp.int32, (SEQ, SEQ), 0)
    j_pos = lax.broadcasted_iota(jnp.int32, (SEQ, SEQ), 1)
    keep = jnp.logical_and(j_pos <= i_pos, j_pos < lenb[0:1, 0:1])
    scale = 1.0 / float(np.sqrt(128.0))
    t_here = 2 * l + h

    def a_self(ld):
        return jnp.logical_and(main, l == ld)

    def a_out(ld, hd):
        return remote(aout.at[hd], ab.at[t_here, hd], a_ss.at[ld, hd], a_rs.at[t_here, hd], device(y, c, z, ld, c))

    def a_in(t, hd):
        return remote(aout.at[hd], ab.at[t, hd], a_ss.at[0, hd], a_rs.at[t, hd], sibling)

    def b_copy(t, hd):
        return remote(ab.at[t, hd], ab.at[t, hd], b_ss.at[t, hd], b_rs.at[t, hd], sibling)

    for hd in range(HEADS):
        rq = rotate(acc[:, hd * HEAD : (hd + 1) * HEAD] * rs)
        s = lax.dot_general(rq, rk, (((1,), (1,)), ((), ())), preferred_element_type=jnp.float32) * scale
        s = jnp.where(keep, s, jnp.float32(-1e30))
        e = jnp.exp(s - jnp.max(s, axis=1, keepdims=True))
        total = jnp.sum(e, axis=1, keepdims=True)
        o = jnp.dot(e.astype(jnp.bfloat16), rv, preferred_element_type=jnp.float32) / total
        o = o.astype(jnp.bfloat16)
        aout[hd] = o
        for ld in (0, 1):
            @pl.when(jnp.logical_not(a_self(ld)))
            def _():
                a_out(ld, hd).start()

        @pl.when(main)
        def _():
            ab[t_here, hd] = o
            b_copy(t_here, hd).start()

    for d in (0, 1):
        g_y_in(d, d).wait_recv()
        g_f(d).start()

    def attended_here(t, hd):
        @pl.when(jnp.logical_and(main, t != t_here))
        def _():
            a_in(t, hd).wait_recv()
            b_copy(t, hd).start()

        @pl.when(jnp.logical_not(main))
        def _():
            b_copy(t, hd).wait_recv()

    def product(zz, groups, heads):
        n = len(heads) * HEAD
        rows_w = pl.ds(heads[0] * HEAD, n)
        a = jnp.concatenate([ab[t, hd] for t in groups for hd in heads], axis=1)
        w = jnp.concatenate(
            [jnp.concatenate([wo[zz, 2 * t, rows_w], wo[zz, 2 * t + 1, rows_w]], axis=1) for t in groups], axis=0
        )
        return jnp.dot(a, w, preferred_element_type=jnp.float32)

    for part in (0, 1):
        heads = (2 * part, 2 * part + 1)
        for hd in heads:
            for t in range(4):
                attended_here(t, hd)

        def out_body(j, _, heads=heads):
            zz = (z + j + NZ - 2) % NZ
            mixed[zz] += product(zz, (0, 1, 2), heads)
            return 0

        if part == 0:
            lax.fori_loop(0, 5, out_body, 0)
            for d in (0, 1):
                for kind in (1, 2):
                    oz_in(3, d, kind).wait_recv()
            far_in.wait_recv()
            lax.fori_loop(5, NZ, out_body, 0)
    for d in (0, 1):
        g_y_in(d, 1 - d).wait_recv()
        g_f_in(d).wait_recv()

    def last_body(zz, _):
        total = mixed[zz] + product(zz, (0, 1, 2), (2, 3)) + product(zz, (3,), (0, 1, 2, 3))
        for hh in (0, 1):
            cols = pl.ds(pl.multiple_of(hh * 1024 + zz * 128, 128), 128)
            out[:, cols] = total[:, hh * 128 : (hh + 1) * 128].astype(jnp.bfloat16)
        return 0

    lax.fori_loop(0, NZ, last_body, 0)

    @pl.when(jnp.logical_not(main))
    def _():
        exchange.wait_send()
        len_out.wait_send()
        tok_copy(x, 0, 2).wait_send()
        tok_copy(x, 1, 2).wait_send()

    for hd in (0, 1):
        @pl.when(jnp.logical_not(jnp.logical_and(source, h == hd)))
        def _():
            ox[hd].wait_send()
    for k in (0, 1):
        tok_copy(pair_x, k, 0).wait_send()
        tok_copy(outer_x, k, 1).wait_send()
        tok_forward(k).wait_send()
    for d in (0, 1):
        for i in range(8):
            w1_y(d, i).wait_send()
        for j in range(5):
            w1_f(d, j).wait_send()
            far_share(yf, c, d, j).wait_send()
        for s in (1, 2, 3, 4):
            w1_z(s, d).wait_send()
            g_z(s, d).wait_send()
        for k in (0, 1):
            g_y(d, k).wait_send()
        for s in (1, 2, 3):
            for kind in (0, 1, 2):
                oz(s, d, kind).wait_send()
        oz(4, d, 0).wait_send()
        g_f(d).wait_send()
    far_out.wait_send()
    share(plane(y, c), 0).wait_send()
    share(plane(yn, c), 1).wait_send()
    share(plane(yp, c), 2).wait_send()

    @pl.when(source)
    def _():
        for q in (1, 2, 3):
            scatter(q).wait_send()
        for d in (0, 1):
            for k in (0, 1):
                oy(d, k).wait_send()

    for k in (0, 1):
        @pl.when(jnp.logical_and(rel == 1, c == 1))
        def _():
            oy(0, k).wait_send()

        @pl.when(jnp.logical_and(rel == 3, c == 0))
        def _():
            oy(1, k).wait_send()

    for hd in range(HEADS):
        for ld in (0, 1):
            @pl.when(jnp.logical_not(a_self(ld)))
            def _():
                a_out(ld, hd).wait_send()

        @pl.when(main)
        def _():
            for t in range(4):
                b_copy(t, hd).wait_send()


def per_device(tokens, norm_gain, q_weight, key_value_weight, output_weight, lengths):
    cosine, sine = rotary_tables()
    dma = pltpu.SemaphoreType.DMA
    vmem = pl.BlockSpec(memory_space=pltpu.VMEM)
    bf16 = jnp.bfloat16
    return pl.pallas_call(
        kernel,
        out_shape=pltpu.VMEM((SEQ, FEATS), bf16),
        in_specs=[pl.BlockSpec(memory_space=pl.ANY)] + [vmem] * 4 + [pl.BlockSpec(memory_space=pltpu.SMEM)] + [vmem] * 2,
        out_specs=vmem,
        scratch_shapes=[
            pltpu.VMEM((SEQ, FEATS), bf16),
            pltpu.VMEM((1, 4 * FEATS), jnp.float32),
            pltpu.VMEM((128, 768), bf16),
            pltpu.VMEM((8, 128), jnp.int32),
            pltpu.VMEM((4, SEQ, FEATS), bf16),
            pltpu.VMEM((64, 128, 768), bf16),
            pltpu.VMEM((NZ + 1, 8, 512, 128), bf16),
            pltpu.VMEM((4, HEADS, SEQ, HEAD), bf16),
            pltpu.VMEM((HEADS, SEQ, HEAD), bf16),
            pltpu.VMEM((8, 128), jnp.int32),
            pltpu.VMEM((SEQ, 768), jnp.float32),
            pltpu.VMEM((SEQ, 128), jnp.float32),
            pltpu.VMEM((SEQ, FEATS), bf16),
            pltpu.VMEM((NZ, SEQ, 256), jnp.float32),
            dma((3, 2)), dma((4, 2)), dma((2,)), dma((6,)), dma((1,)), dma((1,)), dma((1,)), dma((1,)),
            dma((2, 4)), dma((2, 4)), dma((2, 8)), dma((2, 8)), dma((2, 5)), dma((2, 5)), dma((13,)), dma((13,)),
            dma((2,)), dma((8,)), dma((2, 2)), dma((2,)), dma((2, 4, 3)), dma((2, 4, 3)),
            dma((3,)), dma((1,)), dma((2, 4)), dma((2, 4)), dma((2, 3)), dma((2, 3)), dma((1,)), dma((1,)),
            dma((2, HEADS)), dma((4, HEADS)), dma((4, HEADS)), dma((4, HEADS)),
        ],
        compiler_params=pltpu.CompilerParams(
            collective_id=0, has_side_effects=True, vmem_limit_bytes=56 * 2**20
        ),
        cost_estimate=pl.CostEstimate(flops=8 * 10**9, bytes_accessed=4 * 2**20, transcendentals=600000),
    )(tokens, norm_gain, q_weight, key_value_weight, output_weight, lengths, jnp.asarray(cosine), jnp.asarray(sine))


def solution(mesh):
    return jax.shard_map(
        per_device,
        mesh=mesh,
        in_specs=(
            P("dp", "tensor"),
            P(),
            P("dp", "tensor"),
            P("dp", None, "tensor"),
            P("tensor", "dp"),
            P("dp"),
        ),
        out_specs=P("dp", "tensor"),
        check_vma=False,
    )
```
